512 devices in a mesh: ctx: 128 (over y, z, core), tp: 4 (over x).
Axes of the slice: x: 4, y: 8, z: 8, core: 2. Of those that a mesh axis runs over, the one named last changes fastest.
Arguments:
- y_first: bfloat16 [16384, 2048], P('ctx', 'tp'), may hold values from -6 to 6
- x_second: bfloat16 [16384, 2048], P('ctx', 'tp'), may hold values from -6 to 6
- grad_first: bfloat16 [16384, 2048], P('ctx', 'tp'), may hold values from -6 to 6
- grad_second: bfloat16 [16384, 2048], P('ctx', 'tp'), may hold values from -6 to 6
- w_query: bfloat16 [2048, 2048], P('ctx', 'tp'), may hold values from -0.125 to 0.125
- w_key: bfloat16 [2048, 2048], P('ctx', 'tp'), may hold values from -0.125 to 0.125
- w_value: bfloat16 [2048, 2048], P('ctx', 'tp'), may hold values from -0.125 to 0.125
- w_out: bfloat16 [2048, 2048], P('tp', 'ctx'), may hold values from -0.125 to 0.125
- norm_gain: float32 [2048], P('tp'), may hold values from 0.1 to 1.9
Outputs:
- x_first: bfloat16 [16384, 2048], P('ctx', 'tp')
- grad_x_second: bfloat16 [16384, 2048], P('ctx', 'tp')
The draws below stay inside these ranges and needn't reach their ends.
All inputs are finite; a program needn't handle non-finite values.
Results may differ from the reference program's by a relative error of at most 0.015.
Values may be sent and summed in bfloat16 or wider, within the bound.
A program may use at most 192 MiB of HBM per device.

```python
import jax
import jax.numpy as jnp
from jax import lax

D = 2048
HEADS = 16
HEAD = 128
HF = 2048
TOKENS = 16384
N_CTX = 128


def shard_levels(stream_key, shape, shards, least, largest):
    def one(dim, blocks):
        heights = jax.random.uniform(jax.random.fold_in(jax.random.fold_in(stream_key, 6), dim), (blocks,), jnp.float32, least / len(shards), largest / len(shards))
        return jnp.repeat(jnp.exp(heights), shape[dim] // blocks).reshape((-1,) + (1,) * (len(shape) - dim - 1))

    factor_of = one(*shards[0])
    for cut in shards[1:]:
        factor_of = factor_of * one(*cut)
    return factor_of


def normal_values(stream_key, extent, spread, most, split=(), held_as=jnp.bfloat16):
    result = jax.random.normal(stream_key, extent, jnp.float32) * spread
    if len(split) > 0:
        result = shard_levels(stream_key, extent, split, -0.22, 0.18) * result
    return jnp.clip(result, min=-most, max=most).astype(held_as)


def setup_inputs(seed: int = 0) -> dict:
    keys = jax.random.split(jax.random.key(seed), 10)
    y_first = normal_values(keys[0], (TOKENS, D), 1.0, 6.0, ((0, 128), (1, 4)))
    x_second = normal_values(keys[1], (TOKENS, D), 1.0, 6.0, ((0, 128), (1, 4)))
    grad_first = normal_values(keys[2], (TOKENS, D), 1.0, 6.0, ((0, 128), (1, 4)))
    grad_second = normal_values(keys[3], (TOKENS, D), 1.0, 6.0, ((0, 128), (1, 4)))
    w_query = normal_values(keys[4], (D, HF), D ** -0.5, 0.125, ((0, 128), (1, 4)))
    w_key = normal_values(keys[5], (D, HF), D ** -0.5, 0.125, ((0, 128), (1, 4)))
    w_value = normal_values(keys[6], (D, HF), D ** -0.5, 0.125, ((0, 128), (1, 4)))
    w_out = normal_values(keys[7], (HF, D), HF ** -0.5, 0.125, ((0, 4), (1, 128)))
    norm_gain = jnp.clip(1.0 + 0.18 * jax.random.normal(keys[8], (HF,), jnp.float32), 0.1, 1.9)
    return {"y_first": y_first, "x_second": x_second, "grad_first": grad_first, "grad_second": grad_second, "w_query": w_query, "w_key": w_key, "w_value": w_value, "w_out": w_out, "norm_gain": norm_gain}


eps_norm = 1e-06
highest = lax.Precision.HIGHEST

def feature_map(pre):
    return jnp.where(pre > 0, pre + 1.0, jnp.exp(jnp.minimum(pre, 0.0)))

def feature_slope(pre):
    return jnp.where(pre > 0, 1.0, jnp.exp(jnp.minimum(pre, 0.0)))

def rounded(value):
    return lax.optimization_barrier(value.astype(jnp.bfloat16))

def widened(value):
    return value.astype(jnp.float32)

def reference(y_first, x_second, grad_first, grad_second, w_query, w_key, w_value, w_out, norm_gain):
    tok_total = x_second.shape[0]
    block_rows = tok_total // N_CTX
    pre_query = jnp.dot(x_second, w_query, preferred_element_type=jnp.float32)
    pre_key = jnp.dot(x_second, w_key, preferred_element_type=jnp.float32)
    query = feature_map(pre_query).astype(jnp.bfloat16)
    key_feat = feature_map(pre_key).astype(jnp.bfloat16)
    value = jnp.dot(x_second, w_value, preferred_element_type=jnp.float32).astype(jnp.bfloat16)
    block_shape = (N_CTX, block_rows, HEADS, HEAD)
    query_blocks = query.reshape(block_shape)
    key_blocks = key_feat.reshape(block_shape)
    value_blocks = value.reshape(block_shape)
    causal = jnp.arange(block_rows)[:, None] >= jnp.arange(block_rows)[None, :]

    def forward_block(state, block):
        query_b, key_b, value_b = block
        scores = jnp.einsum('lhe,mhe->hlm', widened(query_b), widened(key_b), precision=highest)
        attn_scores = rounded(jnp.where(causal[None], scores, 0.0))
        inner = jnp.einsum('hlm,mhe->lhe', widened(attn_scores), widened(value_b), precision=highest)
        cross = jnp.einsum('lhe,hef->lhf', widened(query_b), state, precision=highest)
        local_state = jnp.einsum('lhe,lhf->hef', widened(key_b), widened(value_b), precision=highest)
        return (state + local_state, (inner + cross, state))
    empty_state = jnp.zeros((HEADS, HEAD, HEAD), jnp.float32)
    final_state, outputs = lax.scan(forward_block, empty_state, (query_blocks, key_blocks, value_blocks))
    attn_out = outputs[0].reshape(tok_total, HEADS, HEAD)
    prior_states = outputs[1]
    rms_scale = jnp.sqrt(lax.optimization_barrier(jnp.mean(attn_out * attn_out, axis=-1, keepdims=True)) + eps_norm)
    unit_out = attn_out / rms_scale
    gain_heads = norm_gain.reshape(HEADS, HEAD)
    normed = (unit_out * gain_heads).astype(jnp.bfloat16).reshape(tok_total, HF)
    mixed_out = jnp.dot(normed, w_out, preferred_element_type=jnp.float32)
    x_first = (widened(y_first) - mixed_out).astype(jnp.bfloat16)
    grad_normed = jnp.dot(grad_first, w_out.T, preferred_element_type=jnp.float32).reshape(tok_total, HEADS, HEAD)
    scaled_grad = grad_normed * gain_heads
    grad_out = ((scaled_grad - unit_out * lax.optimization_barrier(jnp.mean(unit_out * scaled_grad, axis=-1, keepdims=True))) / rms_scale).astype(jnp.bfloat16)
    grad_blocks = grad_out.reshape(block_shape)

    def backward_block(later_state, block):
        query_b, key_b, value_b, grad_b, prior_state = block
        scores = jnp.einsum('lhe,mhe->hlm', widened(query_b), widened(key_b), precision=highest)
        attn_scores = rounded(jnp.where(causal[None], scores, 0.0))
        back_scores = jnp.einsum('lhf,mhf->hlm', widened(grad_b), widened(value_b), precision=highest)
        grad_scores = rounded(jnp.where(causal[None], back_scores, 0.0))
        grad_query = jnp.einsum('hlm,mhe->lhe', widened(grad_scores), widened(key_b), precision=highest)
        grad_query = grad_query + jnp.einsum('lhf,hef->lhe', widened(grad_b), prior_state, precision=highest)
        grad_key = jnp.einsum('hlm,lhe->mhe', widened(grad_scores), widened(query_b), precision=highest)
        grad_key = grad_key + jnp.einsum('mhf,hef->mhe', widened(value_b), later_state, precision=highest)
        grad_value = jnp.einsum('hlm,lhf->mhf', widened(attn_scores), widened(grad_b), precision=highest)
        grad_value = grad_value + jnp.einsum('mhe,hef->mhf', widened(key_b), later_state, precision=highest)
        local_back = jnp.einsum('lhe,lhf->hef', widened(query_b), widened(grad_b), precision=highest)
        return (later_state + local_back, (grad_query, grad_key, grad_value))
    first_state, grads = lax.scan(backward_block, empty_state, (query_blocks, key_blocks, value_blocks, grad_blocks, prior_states), reverse=True)
    grad_query = (grads[0].reshape(tok_total, HF) * feature_slope(pre_query)).astype(jnp.bfloat16)
    grad_key = (grads[1].reshape(tok_total, HF) * feature_slope(pre_key)).astype(jnp.bfloat16)
    grad_value = grads[2].reshape(tok_total, HF).astype(jnp.bfloat16)
    terms = jnp.dot(grad_query, w_query.T, preferred_element_type=jnp.float32)
    terms = terms + jnp.dot(grad_key, w_key.T, preferred_element_type=jnp.float32)
    terms = terms + jnp.dot(grad_value, w_value.T, preferred_element_type=jnp.float32)
    grad_x_second = (widened(grad_second) + terms).astype(jnp.bfloat16)
    return (x_first, grad_x_second)
```

```python
import jax
import jax.numpy as jnp
from jax import lax
from jax.experimental import pallas as pl
from jax.experimental.pallas import tpu as pltpu
from jax.sharding import PartitionSpec as P

MESH = pl.DeviceIdType.MESH
F32 = jnp.float32
BF16 = jnp.bfloat16
HEAD = 128
EPS = 1e-06
RING = 8
K, V, Q, O = 0, 1, 2, 3
FAR_FIRST = (4, 3, 5, 2, 6, 1, 7)


def dot_nn(a, b):
    return jnp.dot(a, b, preferred_element_type=F32)


def dot_nt(a, b):
    return lax.dot_general(a, b, (((1,), (1,)), ((), ())), preferred_element_type=F32)


def dot_tn(a, b):
    return lax.dot_general(a, b, (((0,), (0,)), ((), ())), preferred_element_type=F32)


def kernel(
    y_hbm, x_hbm, g_hbm, gs_hbm, wq_hbm, wk_hbm, wv_hbm, wo_hbm, gain_hbm,
    x_first, grad_x,
    wbuf, xg, y_v, gs_v, gain_v,
    q_v, k_v, v_v, slope_q, slope_k, gn_v, attn_s, back_v, dq_v, inner_v,
    st_src, st_in, st_pref, st_rs, st_row, st_po, st_p,
    own_v, core_out, core_in, hop_out, hop_in,
    loc_sem, wx_s, wx_r, p1_s, p1_r, p2_s, p2_r, xa_s, xa_r, xc_s, xc_r,
    st_s, st_r, rc_s, rc_r, rh_s, rh_r,
):
    ctx = lax.axis_index("ctx")
    x = lax.axis_index("tp")
    c = ctx % 2
    z = (ctx // 2) % RING
    y = ctx // (2 * RING)
    pending = []

    def at(yy, zz):
        return ((yy * RING + zz) * 2 + c, x)

    peer = (ctx + 1 - 2 * c, x)
    xr, xl, xo = (x + 1) % 4, (x + 3) % 4, (x + 2) % 4
    right, left = (ctx, xr), (ctx, xl)

    def remote(src, dst, ss, rs, dev):
        return pltpu.make_async_remote_copy(
            src_ref=src, dst_ref=dst, send_sem=ss, recv_sem=rs, device_id=dev, device_id_type=MESH
        )

    def send(src, dst, ss, rs, dev):
        copy = remote(src, dst, ss, rs, dev)
        copy.start()
        pending.append(copy)

    def arrive(dst, ss, rs):
        remote(dst, dst, ss, rs, peer).wait_recv()

    def drain():
        for copy in pending:
            copy.wait_send()
        pending.clear()

    mine = pl.ds(pl.multiple_of(c * 256, 256), 256)
    theirs = pl.ds(pl.multiple_of(256 - c * 256, 256), 256)
    shards = {K: wk_hbm, V: wv_hbm, Q: wq_hbm, O: wo_hbm}
    local = {}

    def stay(name, src, dst):
        local[name] = pltpu.make_async_copy(src, dst, loc_sem.at[len(local)])
        local[name].start()

    for w in (K, V, Q, O):
        stay(w, shards[w].at[:, mine], wbuf.at[w, y, z, c])
    stay("x", x_hbm, xg.at[0, x, 0])
    stay("g", g_hbm, xg.at[1, x, 0])
    stay("gain", gain_hbm, gain_v)
    stay("y", y_hbm, y_v)
    stay("gs", gs_hbm, gs_v)

    barrier = pltpu.get_barrier_semaphore()
    partners = [peer, right, left]
    partners += [at(y, (z + d) % RING) for d in range(1, RING)]
    partners += [at((y + d) % RING, z) for d in range(1, RING)]
    for dev in partners:
        pl.semaphore_signal(barrier, inc=1, device_id=dev, device_id_type=MESH)
    pl.semaphore_wait(barrier, len(partners))

    for w in (K, V, Q, O):
        send(shards[w].at[:, theirs], wbuf.at[w, y, z, c], wx_s.at[w], wx_r.at[w], peer)

    def gather_x(a, src):
        send(src, xg.at[a, x, 0], xa_s.at[a, 0], xa_r.at[a, 0], right)
        send(src, xg.at[a, x, 0], xa_s.at[a, 1], xa_r.at[a, 1], left)
        send(src, xg.at[a, x, 1], xc_s.at[a, 0], xc_r.at[a, 0], peer)

    lo, hi = pl.ds(0, 64), pl.ds(64, 64)

    def forward_x(a):
        arrive(xg.at[a, xl, 0], xa_s.at[a, 0], xa_r.at[a, 0])
        send(xg.at[a, xl, 0, lo], xg.at[a, xl, 0, lo], xa_s.at[a, 2], xa_r.at[a, 2], right)
        send(xg.at[a, xl, 0], xg.at[a, xl, 1], xc_s.at[a, 1], xc_r.at[a, 1], peer)
        arrive(xg.at[a, xr, 0], xa_s.at[a, 1], xa_r.at[a, 1])
        send(xg.at[a, xr, 0, hi], xg.at[a, xr, 0, hi], xa_s.at[a, 3], xa_r.at[a, 3], left)
        send(xg.at[a, xr, 0], xg.at[a, xr, 1], xc_s.at[a, 2], xc_r.at[a, 2], peer)

    def last_x(a):
        arrive(xg.at[a, xo, 0, lo], xa_s.at[a, 2], xa_r.at[a, 2])
        arrive(xg.at[a, xo, 0, hi], xa_s.at[a, 3], xa_r.at[a, 3])
        send(xg.at[a, xo, 0], xg.at[a, xo, 1], xc_s.at[a, 3], xc_r.at[a, 3], peer)

    def all_x(a):
        for i, src in enumerate((x, xl, xr, xo)):
            arrive(xg.at[a, src, 1], xc_s.at[a, i], xc_r.at[a, i])

    def along_y(w):
        return w in (V, O)

    def phase1(w):
        local[w].wait()
        arrive(wbuf.at[w, y, z, 1 - c], wx_s.at[w], wx_r.at[w])
        for d in FAR_FIRST:
            dev = at((y + d) % RING, z) if along_y(w) else at(y, (z + d) % RING)
            send(wbuf.at[w, y, z], wbuf.at[w, y, z], p1_s.at[w, d], p1_r.at[w, d], dev)

    def phase1_done(w):
        for d in FAR_FIRST:
            src = (RING - d) % RING
            dst = wbuf.at[w, (y + src) % RING, z] if along_y(w) else wbuf.at[w, y, (z + src) % RING]
            arrive(dst, p1_s.at[w, d], p1_r.at[w, d])

    def piece(w, index, half):
        part = pl.ds(half * 4, 4)
        return wbuf.at[w, part, index] if along_y(w) else wbuf.at[w, index, part]

    def ring(w, step):
        p = z if along_y(w) else y
        if along_y(w):
            ahead, behind = at(y, (z + 1) % RING), at(y, (z + 7) % RING)
        else:
            ahead, behind = at((y + 1) % RING, z), at((y + 7) % RING, z)
        for way, (dev, index) in enumerate(
            ((ahead, (p + RING - step) % RING), (behind, (p + step) % RING))
        ):
            for half in (0, 1) if way == 0 else (1, 0):
                block = piece(w, index, half)
                if step > 0 and not (step == 4 and half != way):
                    prev = (w, way, step - 1, half)
                    arrive(block, p2_s.at[prev], p2_r.at[prev])
                if step < 3 or (step == 3 and half == way):
                    this = (w, way, step, half)
                    send(block, block, p2_s.at[this], p2_r.at[this], dev)

    def state_out(turn, states):
        for h in range(2):
            st_src[turn, :, h] = states[h].astype(BF16).reshape(RING, 16, HEAD)
        st_in[turn, z] = st_src[turn, z]
        for d in FAR_FIRST:
            zt = (z + d) % RING
            send(st_src.at[turn, zt], st_in.at[turn, z], st_s.at[turn, 0, d], st_r.at[turn, 0, d], at(y, zt))

    def state_rows(turn):
        for d in FAR_FIRST:
            arrive(st_in.at[turn, (z + RING - d) % RING], st_s.at[turn, 0, d], st_r.at[turn, 0, d])
        total = jnp.zeros((2, 16, HEAD), F32)
        for i in range(RING) if turn == 0 else range(RING - 1, -1, -1):
            st_pref[i] = total
            total = total + st_in[turn, i].astype(F32)
        st_rs[turn] = total.astype(BF16)
        for d in FAR_FIRST:
            send(st_rs.at[turn], st_row.at[turn, y], st_s.at[turn, 1, d], st_r.at[turn, 1, d], at((y + d) % RING, z))
        st_row[turn, y] = st_rs[turn]

    def state_back(turn):
        for d in FAR_FIRST:
            arrive(st_row.at[turn, (y + RING - d) % RING], st_s.at[turn, 1, d], st_r.at[turn, 1, d])
        total = jnp.zeros((2, 16, HEAD), F32)
        for i in range(RING):
            use = (i < y) if turn == 0 else (i > y)
            total = total + jnp.where(use, st_row[turn, i].astype(F32), 0.0)
        for i in range(RING):
            st_po[turn, i] = (total + st_pref[i]).astype(BF16)
        st_p[turn, z] = st_po[turn, z]
        for d in FAR_FIRST:
            zt = (z + d) % RING
            send(st_po.at[turn, zt], st_p.at[turn, z], st_s.at[turn, 2, d], st_r.at[turn, 2, d], at(y, zt))

    def state_done(turn):
        for d in FAR_FIRST:
            arrive(st_p.at[turn, (z + RING - d) % RING], st_s.at[turn, 2, d], st_r.at[turn, 2, d])

    def state(turn, h):
        return st_p[turn, :, h].reshape(HEAD, HEAD)

    targets = {1: xr, 2: xo, 3: xl, 0: x}

    def rows_of(w, target):
        return wbuf[w, pl.ds(target * 2, 2)].reshape(512, 256)

    def sum_cores(a, product):
        for d in (2, 1, 3, 0):
            block = product(targets[d])
            core_out[a, d] = block[128:].astype(BF16)
            send(core_out.at[a, d], core_in.at[a, d], rc_s.at[a, d], rc_r.at[a, d], peer)
            own_v[d] = block[:128]

    def both(a, d):
        arrive(core_in.at[a, d], rc_s.at[a, d], rc_r.at[a, d])
        return own_v[d] + core_in[a, d].astype(F32)

    def hop(a, d, part, dev, i):
        send(hop_out.at[a, d, part], hop_in.at[a, d, part], rh_s.at[a, i], rh_r.at[a, i], dev)

    def landed(a, d, part, i):
        arrive(hop_in.at[a, d, part], rh_s.at[a, i], rh_r.at[a, i])

    def sum_first(a):
        hop_out[a, 2] = both(a, 2).astype(BF16)
        hop(a, 2, lo, right, 0)
        hop(a, 2, hi, left, 1)
        block = both(a, 1)
        hop_out[a, 1, 64:] = block[64:].astype(BF16)
        hop(a, 1, hi, right, 2)
        own_v[1] = block
        block = both(a, 3)
        hop_out[a, 3, :64] = block[:64].astype(BF16)
        hop(a, 3, lo, left, 3)
        own_v[3] = block

    def sum_second(a):
        landed(a, 2, lo, 0)
        hop_out[a, 1, :64] = (own_v[1, :64] + hop_in[a, 2, :64].astype(F32)).astype(BF16)
        hop(a, 1, lo, right, 4)
        landed(a, 2, hi, 1)
        hop_out[a, 3, 64:] = (own_v[3, 64:] + hop_in[a, 2, 64:].astype(F32)).astype(BF16)
        hop(a, 3, hi, left, 5)

    def sum_last(a):
        total = both(a, 0)
        landed(a, 1, hi, 2)
        landed(a, 3, lo, 3)
        landed(a, 1, lo, 4)
        landed(a, 3, hi, 5)
        return total + hop_in[a, 1].astype(F32) + hop_in[a, 3].astype(F32)

    def project(a, w):
        total = None
        for i in range(4):
            part = dot_nn(xg[a, i].reshape(256, 512), wbuf[w, 2 * i : 2 * i + 2].reshape(512, 256))
            total = part if total is None else total + part
        return total

    def feature(pre):
        return jnp.where(pre > 0, pre + 1.0, jnp.exp(jnp.minimum(pre, 0.0)))

    head = [slice(0, HEAD), slice(HEAD, 2 * HEAD)]
    place = [(lax.broadcasted_iota(jnp.int32, (256, 256), i) + c * 128) % 256 for i in range(2)]
    causal = place[0] >= place[1]

    phase1(K)
    phase1(V)
    gather_x(0, x_hbm)
    phase1_done(K)
    ring(K, 0)
    phase1_done(V)
    ring(V, 0)
    phase1(Q)
    phase1(O)
    ring(K, 1)
    ring(V, 1)
    forward_x(0)
    gather_x(1, g_hbm)
    ring(K, 2)
    ring(V, 2)
    last_x(0)
    phase1_done(Q)
    phase1_done(O)
    ring(K, 3)
    ring(V, 3)
    ring(Q, 0)
    ring(O, 0)
    forward_x(1)
    local["x"].wait()
    all_x(0)
    ring(K, 4)
    feat = feature(project(0, K))
    slope_k[...] = jnp.minimum(feat, 1.0)
    k_v[...] = feat.astype(BF16)
    ring(V, 4)
    v_v[...] = project(0, V).astype(BF16)
    state_out(0, [dot_tn(k_v[:, s], v_v[:, s]) for s in head])
    last_x(1)
    ring(Q, 1)
    ring(O, 1)
    state_rows(0)
    ring(Q, 2)
    ring(O, 2)
    state_back(0)
    ring(Q, 3)
    ring(O, 3)
    drain()
    local["g"].wait()
    local["gain"].wait()
    all_x(1)
    ring(Q, 4)
    feat = feature(project(0, Q))
    slope_q[...] = jnp.minimum(feat, 1.0)
    q_v[...] = feat.astype(BF16)
    for h, s in enumerate(head):
        scores = jnp.where(causal, dot_nt(q_v[:, s], k_v[:, s]), 0.0).astype(BF16)
        attn_s[h] = scores
        inner_v[:, s] = dot_nn(scores, v_v[:, s])
    ring(O, 4)
    gain = jnp.where(c == 0, gain_v[:, :256], gain_v[:, 256:])
    gn_v[...] = project(1, O) * gain

    state_done(0)
    normed = []
    backs = []
    for h, s in enumerate(head):
        attn = inner_v[:, s] + dot_nn(q_v[:, s], state(0, h))
        scale = lax.rsqrt(jnp.mean(attn * attn, axis=-1, keepdims=True) + EPS)
        unit = attn * scale
        normed.append((unit * gain[:, s]).astype(BF16))
        scaled = gn_v[:, s]
        back = ((scaled - unit * jnp.mean(unit * scaled, axis=-1, keepdims=True)) * scale).astype(BF16)
        back_v[:, s] = back
        backs.append(dot_tn(q_v[:, s], back))
    state_out(1, backs)
    normed = jnp.concatenate(normed, axis=1)
    sum_cores(0, lambda target: dot_nt(normed, rows_of(O, target)))
    sum_first(0)
    state_rows(1)
    for h, s in enumerate(head):
        back = back_v[:, s]
        gs = jnp.where(causal, dot_nt(back, v_v[:, s]), 0.0).astype(BF16)
        gq = dot_nn(gs, k_v[:, s]) + dot_nt(back, state(0, h))
        dq_v[0, :, s] = (gq * slope_q[:, s]).astype(BF16)
        gn_v[:, s] = dot_tn(gs, q_v[:, s])
        inner_v[:, s] = dot_tn(attn_s[h], back)
    state_back(1)
    sum_second(0)
    local["y"].wait()
    x_first[...] = (y_v[...].astype(F32) - sum_last(0)).astype(BF16)
    drain()

    state_done(1)
    for h, s in enumerate(head):
        later = state(1, h)
        gk = gn_v[:, s] + dot_nt(v_v[:, s], later)
        dq_v[1, :, s] = (gk * slope_k[:, s]).astype(BF16)
        dq_v[2, :, s] = (inner_v[:, s] + dot_nn(k_v[:, s], later)).astype(BF16)
    sum_cores(
        1,
        lambda target: dot_nt(dq_v[0], rows_of(Q, target))
        + dot_nt(dq_v[1], rows_of(K, target))
        + dot_nt(dq_v[2], rows_of(V, target)),
    )
    sum_first(1)
    sum_second(1)
    local["gs"].wait()
    grad_x[...] = (gs_v[...].astype(F32) + sum_last(1)).astype(BF16)
    drain()


def per_device(
    y_first, x_second, grad_first, grad_second, w_query, w_key, w_value, w_out, norm_gain
):
    dma = pltpu.SemaphoreType.DMA
    vm = pltpu.VMEM
    scratch = [
        vm((4, 8, 8, 2, 16, 256), BF16),
        vm((2, 4, 2, 128, 512), BF16),
        vm((128, 512), BF16),
        vm((128, 512), BF16),
        vm((1, 512), F32),
        vm((256, 256), BF16),
        vm((256, 256), BF16),
        vm((256, 256), BF16),
        vm((256, 256), F32),
        vm((256, 256), F32),
        vm((256, 256), F32),
        vm((2, 256, 256), BF16),
        vm((256, 256), BF16),
        vm((3, 256, 256), BF16),
        vm((256, 256), F32),
        vm((2, 8, 2, 16, 128), BF16),
        vm((2, 8, 2, 16, 128), BF16),
        vm((8, 2, 16, 128), F32),
        vm((2, 2, 16, 128), BF16),
        vm((2, 8, 2, 16, 128), BF16),
        vm((2, 8, 2, 16, 128), BF16),
        vm((2, 8, 2, 16, 128), BF16),
        vm((4, 128, 512), F32),
        vm((2, 4, 128, 512), BF16),
        vm((2, 4, 128, 512), BF16),
        vm((2, 4, 128, 512), BF16),
        vm((2, 4, 128, 512), BF16),
        dma((9,)),
        dma((4,)), dma((4,)),
        dma((4, 8)), dma((4, 8)),
        dma((4, 2, 4, 2)), dma((4, 2, 4, 2)),
        dma((2, 4)), dma((2, 4)),
        dma((2, 4)), dma((2, 4)),
        dma((2, 3, 8)), dma((2, 3, 8)),
        dma((2, 4)), dma((2, 4)),
        dma((2, 6)), dma((2, 6)),
    ]
    out = jax.ShapeDtypeStruct((128, 512), BF16)
    anywhere = pl.BlockSpec(memory_space=pl.ANY)
    return pl.pallas_call(
        kernel,
        out_shape=(out, out),
        in_specs=[anywhere] * 9,
        out_specs=(pl.BlockSpec(memory_space=pltpu.VMEM),) * 2,
        scratch_shapes=scratch,
        compiler_params=pltpu.CompilerParams(
            collective_id=0, has_side_effects=True, vmem_limit_bytes=48 * 2**20
        ),
        cost_estimate=pl.CostEstimate(
            flops=4_000_000_000, bytes_accessed=10_000_000, transcendentals=200_000
        ),
    )(
        y_first, x_second, grad_first, grad_second,
        w_query, w_key, w_value, w_out.T, norm_gain.reshape(1, 512),
    )


def solution(mesh):
    in_specs = (P("ctx", "tp"),) * 7 + (P("tp", "ctx"), P("tp"))
    out_specs = (P("ctx", "tp"), P("ctx", "tp"))
    return jax.shard_map(
        per_device, mesh=mesh, in_specs=in_specs, out_specs=out_specs, check_vma=False
    )
```

```python
import jax
import jax.numpy as jnp
from jax import lax
from jax.experimental import pallas as pl
from jax.experimental.pallas import tpu as pltpu
from jax.sharding import PartitionSpec as P

MESH = pl.DeviceIdType.MESH
F32 = jnp.float32
BF16 = jnp.bfloat16
HEAD = 128
EPS = 1e-06
RING = 8
K, V, Q, O = 0, 1, 2, 3
FAR_FIRST = (4, 3, 5, 2, 6, 1, 7)

S_SWAP, S_FIRST, S_SECOND, S_X, S_XC, S_STATE, S_CORE, S_HOP = 0, 1, 5, 9, 11, 13, 19, 21
SENT = 23
R_SWAP, R_FIRST, R_SECOND, R_X, R_XC, R_STATE, R_CORE, R_HOP = 0, 4, 36, 148, 160, 162, 168, 176
ARRIVED = 188


def dot_nn(a, b):
    return jnp.dot(a, b, preferred_element_type=F32)


def dot_nt(a, b):
    return lax.dot_general(a, b, (((1,), (1,)), ((), ())), preferred_element_type=F32)


def dot_tn(a, b):
    return lax.dot_general(a, b, (((0,), (0,)), ((), ())), preferred_element_type=F32)


def kernel(
    y_hbm, x_hbm, g_hbm, gs_hbm, wq_hbm, wk_hbm, wv_hbm, wo_hbm, gain_hbm,
    x_first, grad_x,
    wbuf, xg, y_v, gs_v, gain_v,
    q_v, k_v, v_v, slope_q, slope_k, gn_v, attn_s, back_v, normed_v, dq_v, inner_v,
    st_src, st_in, st_pref, st_rs, st_row, st_po, st_p, state_v, early_v,
    own_v, core_out, core_in, hop_out, hop_in,
    loc_sem, sent, arrived,
):
    ctx = lax.axis_index("ctx")
    x = lax.axis_index("tp")
    c = ctx % 2
    z = (ctx // 2) % RING
    y = ctx // (2 * RING)

    def at(yy, zz):
        return ((yy * RING + zz) * 2 + c, x)

    peer = (ctx + 1 - 2 * c, x)
    xr, xl, xo = (x + 1) % 4, (x + 3) % 4, (x + 2) % 4
    right, left = (ctx, xr), (ctx, xl)

    def remote(src, dst, ss, rs, dev):
        return pltpu.make_async_remote_copy(
            src_ref=src, dst_ref=dst, send_sem=ss, recv_sem=rs, device_id=dev, device_id_type=MESH
        )

    def send(src, dst, ss, rs, dev):
        remote(src, dst, ss, rs, dev).start()

    def arrive(dst, rs):
        remote(dst, dst, sent.at[0], rs, peer).wait_recv()

    def left_here(src, ss):
        remote(src, src, ss, arrived.at[0], peer).wait_send()

    mine = pl.ds(pl.multiple_of(c * 256, 256), 256)
    theirs = pl.ds(pl.multiple_of(256 - c * 256, 256), 256)
    shards = {K: wk_hbm, V: wv_hbm, Q: wq_hbm, O: wo_hbm}
    local = {}

    def stay(name, src, dst):
        local[name] = pltpu.make_async_copy(src, dst, loc_sem.at[len(local)])
        local[name].start()

    for w in (K, V, Q, O):
        stay(w, shards[w].at[:, mine], wbuf.at[w, y, z, c])
    stay("x", x_hbm, xg.at[0, x, 0])
    stay("g", g_hbm, xg.at[1, x, 0])
    stay("gain", gain_hbm, gain_v)
    stay("y", y_hbm, y_v)
    stay("gs", gs_hbm, gs_v)

    barrier = pltpu.get_barrier_semaphore()
    partners = [peer, right, left]
    partners += [at(y, (z + d) % RING) for d in range(1, RING)]
    partners += [at((y + d) % RING, z) for d in range(1, RING)]
    for dev in partners:
        pl.semaphore_signal(barrier, inc=1, device_id=dev, device_id_type=MESH)
    pl.semaphore_wait(barrier, len(partners))

    lo, hi = pl.ds(0, 64), pl.ds(64, 64)

    def x_hop(a, i, src, owner, part, dev):
        send(src.at[part], xg.at[a, owner, 0, part], sent.at[S_X + a], arrived.at[R_X + 6 * a + i], dev)

    def x_share(a, src, owner):
        send(src, xg.at[a, owner, 1], sent.at[S_XC + a], arrived.at[R_XC + a], peer)

    def x_here(a, i, owner, part):
        arrive(xg.at[a, owner, 0, part], arrived.at[R_X + 6 * a + i])

    def gather_x(a, src):
        x_hop(a, 0, src, x, lo, right)
        x_hop(a, 1, src, x, hi, left)
        x_hop(a, 2, src, x, hi, right)
        x_hop(a, 3, src, x, lo, left)
        x_share(a, src, x)

    def forward_x(a):
        x_here(a, 0, xl, lo)
        x_hop(a, 4, xg.at[a, xl, 0], xl, lo, right)
        x_here(a, 1, xr, hi)
        x_hop(a, 5, xg.at[a, xr, 0], xr, hi, left)

    def share_x(a):
        x_here(a, 2, xl, hi)
        x_share(a, xg.at[a, xl, 0], xl)
        x_here(a, 3, xr, lo)
        x_share(a, xg.at[a, xr, 0], xr)

    def last_x(a):
        x_here(a, 4, xo, lo)
        x_here(a, 5, xo, hi)
        x_share(a, xg.at[a, xo, 0], xo)

    def all_x(a):
        arrive(xg.at[a, :, 1], arrived.at[R_XC + a])

    def x_sent(a):
        left_here(xg.at[a, pl.ds(0, 3), 0], sent.at[S_X + a])
        left_here(xg.at[a, :, 1], sent.at[S_XC + a])

    def along_y(w):
        return w in (V, O)

    def first(w, shift):
        return at((y + shift) % RING, z) if along_y(w) else at(y, (z + shift) % RING)

    def second(w, shift):
        return at(y, (z + shift) % RING) if along_y(w) else at((y + shift) % RING, z)

    def block(w, one, two):
        if along_y(w):
            return wbuf.at[w, (y + one) % RING, (z + two) % RING]
        return wbuf.at[w, (y + two) % RING, (z + one) % RING]

    def shard_ready(w):
        local[w].wait()
        arrive(wbuf.at[w, y, z, 1 - c], arrived.at[R_SWAP + w])

    def spread(w):
        shard_ready(w)
        for d in FAR_FIRST:
            send(block(w, 0, 0), block(w, 0, 0), sent.at[S_FIRST + w], arrived.at[R_FIRST + 8 * w], first(w, d))

    def spread_done(w):
        arrive(wbuf.at[w, 0, pl.ds(0, 7)], arrived.at[R_FIRST + 8 * w])

    def ring_first(w, step):
        if step == 0:
            shard_ready(w)
        for way, sign in enumerate((-1, 1)):
            ref = block(w, (sign * step) % RING, 0)
            sem = R_FIRST + 8 * w + 4 * way + step
            if step > 0:
                arrive(ref.at[way] if step == 4 else ref, arrived.at[sem - 1])
            if step < 4:
                out = ref.at[way] if step == 3 else ref
                send(out, out, sent.at[S_FIRST + w], arrived.at[sem], first(w, -sign))

    def chunk(w, part, two):
        part = pl.ds(2 * part, 2)
        if along_y(w):
            return wbuf.at[w, part, (z + two) % RING]
        return wbuf.at[w, (y + two) % RING, part]

    def ring_second(w, step, i):
        for way, sign in enumerate((-1, 1)):
            ref = chunk(w, 3 - i if way else i, (sign * step) % RING)
            sem = R_SECOND + (w * 2 + way) * 14 + 4 * step + i
            if step > 0 and not (step == 4 and i > 1):
                arrive(ref, arrived.at[sem - 4])
            if step < 3 or (step == 3 and i < 2):
                send(ref, ref, sent.at[S_SECOND + w], arrived.at[sem], second(w, -sign))

    def weight_sent(w):
        left_here(wbuf.at[w, 0, pl.ds(0, 7)], sent.at[S_FIRST + w])
        left_here(wbuf.at[w, pl.ds(0, 7)], sent.at[S_SECOND + w])

    def exchange(turn, stage, src, dst, dev):
        index = 3 * turn + stage
        for d in FAR_FIRST:
            send(src(d), dst.at[turn, d], sent.at[S_STATE + index], arrived.at[R_STATE + index], dev(d))

    def exchanged(turn, stage, dst):
        arrive(dst.at[turn, pl.ds(1, 7)], arrived.at[R_STATE + 3 * turn + stage])

    def state_out(turn, states):
        for h in range(2):
            st_src[turn, :, h] = states[h].astype(BF16).reshape(RING, 16, HEAD)
        exchange(turn, 0, lambda d: st_src.at[turn, (z + d) % RING], st_in, lambda d: at(y, (z + d) % RING))
        st_in[turn, 0] = st_src[turn, z]

    def state_rows(turn):
        exchanged(turn, 0, st_in)
        total = jnp.zeros((2, 16, HEAD), F32)
        parts = []
        for i in range(RING) if turn == 0 else range(RING - 1, -1, -1):
            parts.append((i, total))
            total = total + st_in[turn, (z + RING - i) % RING].astype(F32)
        st_rs[turn] = total.astype(BF16)
        exchange(turn, 1, lambda d: st_rs.at[turn], st_row, lambda d: at((y + d) % RING, z))
        for i, part in parts:
            st_pref[i] = part

    def state_back(turn):
        exchanged(turn, 1, st_row)
        total = jnp.zeros((2, 16, HEAD), F32)
        for d in range(1, RING):
            use = (y >= d) if turn == 0 else (y < d)
            total = total + jnp.where(use, st_row[turn, d].astype(F32), 0.0)
        for i in range(RING):
            st_po[turn, i] = (total + st_pref[i]).astype(BF16)
        exchange(turn, 2, lambda d: st_po.at[turn, (z + d) % RING], st_p, lambda d: at(y, (z + d) % RING))
        st_p[turn, 0] = st_po[turn, z]

    def state_done(turn):
        exchanged(turn, 2, st_p)
        for j in range(RING):
            part = st_p[turn, (z + RING - j) % RING]
            for h in range(2):
                state_v[turn, h, pl.ds(16 * j, 16)] = part[h]

    def state(turn, h):
        return state_v[turn, h]

    def state_sent(turn):
        for stage in range(3):
            left_here(st_p.at[turn, pl.ds(1, 7)], sent.at[S_STATE + 3 * turn + stage])

    targets = {1: xr, 2: xo, 3: xl, 0: x}

    def rows_of(w, target):
        return wbuf[w, pl.ds(target * 2, 2)].reshape(512, 256)

    def sum_cores(a, product):
        for d in (2, 1, 3, 0):
            piece = product(d)
            core_out[a, d] = piece[128:].astype(BF16)
            send(core_out.at[a, d], core_in.at[a, d], sent.at[S_CORE + a], arrived.at[R_CORE + 4 * a + d], peer)
            own_v[d] = piece[:128]

    def both(a, d):
        arrive(core_in.at[a, d], arrived.at[R_CORE + 4 * a + d])
        return own_v[d] + core_in[a, d].astype(F32)

    def hop(a, d, part, dev, i):
        send(hop_out.at[a, d, part], hop_in.at[a, d, part], sent.at[S_HOP + a], arrived.at[R_HOP + 6 * a + i], dev)

    def landed(a, d, part, i):
        arrive(hop_in.at[a, d, part], arrived.at[R_HOP + 6 * a + i])

    def sum_first(a):
        hop_out[a, 2] = both(a, 2).astype(BF16)
        hop(a, 2, lo, right, 0)
        hop(a, 2, hi, left, 1)
        block = both(a, 1)
        hop_out[a, 1, 64:] = block[64:].astype(BF16)
        hop(a, 1, hi, right, 2)
        own_v[1] = block
        block = both(a, 3)
        hop_out[a, 3, :64] = block[:64].astype(BF16)
        hop(a, 3, lo, left, 3)
        own_v[3] = block

    def sum_second(a):
        landed(a, 2, lo, 0)
        hop_out[a, 1, :64] = (own_v[1, :64] + hop_in[a, 2, :64].astype(F32)).astype(BF16)
        hop(a, 1, lo, right, 4)
        landed(a, 2, hi, 1)
        hop_out[a, 3, 64:] = (own_v[3, 64:] + hop_in[a, 2, 64:].astype(F32)).astype(BF16)
        hop(a, 3, hi, left, 5)

    def sum_last(a):
        total = both(a, 0)
        landed(a, 1, hi, 2)
        landed(a, 3, lo, 3)
        landed(a, 1, lo, 4)
        landed(a, 3, hi, 5)
        return total + hop_in[a, 1].astype(F32) + hop_in[a, 3].astype(F32)

    def sums_sent(a):
        left_here(core_out.at[a], sent.at[S_CORE + a])
        left_here(hop_out.at[a, pl.ds(1, 3)], sent.at[S_HOP + a])

    def project(a, w):
        total = None
        for i in range(4):
            part = dot_nn(xg[a, i].reshape(256, 512), wbuf[w, 2 * i : 2 * i + 2].reshape(512, 256))
            total = part if total is None else total + part
        return total

    def feature(pre):
        return jnp.where(pre > 0, pre + 1.0, jnp.exp(jnp.minimum(pre, 0.0)))

    head = [slice(0, HEAD), slice(HEAD, 2 * HEAD)]
    place = [(lax.broadcasted_iota(jnp.int32, (256, 256), i) + c * 128) % 256 for i in range(2)]
    causal = place[0] >= place[1]

    for w in (K, V, Q, O):
        send(shards[w].at[:, theirs], wbuf.at[w, y, z, c], sent.at[S_SWAP], arrived.at[R_SWAP + w], peer)

    gather_x(0, x_hbm)
    spread(K)
    spread(V)
    gather_x(1, g_hbm)

    def serve(pair, step, pieces=range(4)):
        for i in pieces:
            for w in pair:
                ring_second(w, step, i)

    def serve_first(step):
        for w in (Q, O):
            ring_first(w, step)

    spread_done(K)
    spread_done(V)
    serve((K, V), 0)
    serve_first(0)
    forward_x(0)
    serve((K, V), 1)
    serve_first(1)
    share_x(0)
    serve((K, V), 2)
    serve_first(2)
    last_x(0)
    serve((K, V), 3)
    serve_first(3)
    serve_first(4)
    serve((Q, O), 0)
    local["x"].wait()
    all_x(0)
    serve((K, V), 4)
    feat = feature(project(0, K))
    slope_k[...] = jnp.minimum(feat, 1.0)
    k_v[...] = feat.astype(BF16)
    v_v[...] = project(0, V).astype(BF16)
    state_out(0, [dot_tn(k_v[:, s], v_v[:, s]) for s in head])
    serve((Q, O), 1)
    forward_x(1)
    share_x(1)
    state_rows(0)
    serve((Q, O), 2)
    last_x(1)
    state_back(0)
    serve((Q, O), 3)
    local["g"].wait()
    local["gain"].wait()
    all_x(1)
    serve((Q, O), 4)
    feat = feature(project(0, Q))
    slope_q[...] = jnp.minimum(feat, 1.0)
    q_v[...] = feat.astype(BF16)
    gain = jnp.where(c == 0, gain_v[:, :256], gain_v[:, 256:])
    gn_v[...] = project(1, O) * gain
    for h, s in enumerate(head):
        scores = jnp.where(causal, dot_nt(q_v[:, s], k_v[:, s]), 0.0).astype(BF16)
        attn_s[h] = scores
        inner_v[:, s] = dot_nn(scores, v_v[:, s])

    state_done(0)
    backs = []
    for h, s in enumerate(head):
        attn = inner_v[:, s] + dot_nn(q_v[:, s], state(0, h))
        scale = lax.rsqrt(jnp.mean(attn * attn, axis=-1, keepdims=True) + EPS)
        unit = attn * scale
        scaled = gn_v[:, s]
        back = ((scaled - unit * jnp.mean(unit * scaled, axis=-1, keepdims=True)) * scale).astype(BF16)
        back_v[:, s] = back
        backs.append(dot_tn(q_v[:, s], back))
        normed_v[:, s] = (unit * gain[:, s]).astype(BF16)
    state_out(1, backs)
    normed = normed_v[...]
    sum_cores(0, lambda d: dot_nt(normed, rows_of(O, targets[d])))
    sum_first(0)
    state_rows(1)
    for h, s in enumerate(head):
        back = back_v[:, s]
        gs = jnp.where(causal, dot_nt(back, v_v[:, s]), 0.0).astype(BF16)
        gq = dot_nn(gs, k_v[:, s]) + dot_nt(back, state(0, h))
        dq_v[0, :, s] = (gq * slope_q[:, s]).astype(BF16)
        gn_v[:, s] = dot_tn(gs, q_v[:, s])
        inner_v[:, s] = dot_tn(attn_s[h], back)
    state_back(1)
    sum_second(0)
    for d in range(4):
        early_v[d] = dot_nt(dq_v[0], rows_of(Q, targets[d]))
    local["y"].wait()
    x_first[...] = (y_v[...].astype(F32) - sum_last(0)).astype(BF16)
    left_here(wbuf.at[0, 0, pl.ds(0, 4), 0], sent.at[S_SWAP])
    for w in (K, V, Q, O):
        weight_sent(w)
    x_sent(0)
    x_sent(1)
    state_sent(0)
    sums_sent(0)

    state_done(1)
    for h, s in enumerate(head):
        later = state(1, h)
        gk = gn_v[:, s] + dot_nt(v_v[:, s], later)
        dq_v[1, :, s] = (gk * slope_k[:, s]).astype(BF16)
        dq_v[2, :, s] = (inner_v[:, s] + dot_nn(k_v[:, s], later)).astype(BF16)
    sum_cores(
        1,
        lambda d: early_v[d]
        + dot_nt(dq_v[1], rows_of(K, targets[d]))
        + dot_nt(dq_v[2], rows_of(V, targets[d])),
    )
    sum_first(1)
    sum_second(1)
    local["gs"].wait()
    grad_x[...] = (gs_v[...].astype(F32) + sum_last(1)).astype(BF16)
    state_sent(1)
    sums_sent(1)


def per_device(
    y_first, x_second, grad_first, grad_second, w_query, w_key, w_value, w_out, norm_gain
):
    dma = pltpu.SemaphoreType.DMA
    vm = pltpu.VMEM
    scratch = [
        vm((4, 8, 8, 2, 16, 256), BF16),
        vm((2, 4, 2, 128, 512), BF16),
        vm((128, 512), BF16),
        vm((128, 512), BF16),
        vm((1, 512), F32),
        vm((256, 256), BF16),
        vm((256, 256), BF16),
        vm((256, 256), BF16),
        vm((256, 256), F32),
        vm((256, 256), F32),
        vm((256, 256), F32),
        vm((2, 256, 256), BF16),
        vm((256, 256), BF16),
        vm((256, 256), BF16),
        vm((3, 256, 256), BF16),
        vm((256, 256), F32),
        vm((2, 8, 2, 16, 128), BF16),
        vm((2, 8, 2, 16, 128), BF16),
        vm((8, 2, 16, 128), F32),
        vm((2, 2, 16, 128), BF16),
        vm((2, 8, 2, 16, 128), BF16),
        vm((2, 8, 2, 16, 128), BF16),
        vm((2, 8, 2, 16, 128), BF16),
        vm((2, 2, 128, 128), BF16),
        vm((4, 256, 512), F32),
        vm((4, 128, 512), F32),
        vm((2, 4, 128, 512), BF16),
        vm((2, 4, 128, 512), BF16),
        vm((2, 4, 128, 512), BF16),
        vm((2, 4, 128, 512), BF16),
        dma((9,)),
        dma((SENT,)),
        dma((ARRIVED,)),
    ]
    out = jax.ShapeDtypeStruct((128, 512), BF16)
    anywhere = pl.BlockSpec(memory_space=pl.ANY)
    return pl.pallas_call(
        kernel,
        out_shape=(out, out),
        in_specs=[anywhere] * 9,
        out_specs=(pl.BlockSpec(memory_space=pltpu.VMEM),) * 2,
        scratch_shapes=scratch,
        compiler_params=pltpu.CompilerParams(
            collective_id=0, has_side_effects=True, vmem_limit_bytes=63_400_000
        ),
        cost_estimate=pl.CostEstimate(
            flops=4_000_000_000, bytes_accessed=10_000_000, transcendentals=200_000
        ),
    )(
        y_first, x_second, grad_first, grad_second,
        w_query, w_key, w_value, w_out.T, norm_gain.reshape(1, 512),
    )


def solution(mesh):
    in_specs = (P("ctx", "tp"),) * 7 + (P("tp", "ctx"), P("tp"))
    out_specs = (P("ctx", "tp"), P("ctx", "tp"))
    return jax.shard_map(
        per_device, mesh=mesh, in_specs=in_specs, out_specs=out_specs, check_vma=False
    )
```

```python
import jax
import jax.numpy as jnp
from jax import lax
from jax.experimental import pallas as pl
from jax.experimental.pallas import tpu as pltpu
from jax.sharding import PartitionSpec as P

MESH = pl.DeviceIdType.MESH
F32 = jnp.float32
BF16 = jnp.bfloat16
HEAD = 128
EPS = 1e-06
RING = 8
K, V, Q, O = 0, 1, 2, 3
FAR_FIRST = (4, 3, 5, 2, 6, 1, 7)

S_SWAP, S_FIRST, S_SECOND, S_X, S_XC, S_STATE, S_CORE, S_HOP = 0, 1, 5, 9, 11, 13, 19, 21
SENT = 23
CHUNKS = (4, 4, 2, 2)
R_SECOND = (22, 50, 78, 92)
R_SWAP, R_FIRST, R_X, R_XC, R_STATE, R_CORE, R_HOP = 0, 4, 106, 118, 120, 126, 134
ARRIVED = 146


def dot_nn(a, b):
    return jnp.dot(a, b, preferred_element_type=F32)


def dot_nt(a, b):
    return lax.dot_general(a, b, (((1,), (1,)), ((), ())), preferred_element_type=F32)


def dot_tn(a, b):
    return lax.dot_general(a, b, (((0,), (0,)), ((), ())), preferred_element_type=F32)


def kernel(
    y_hbm, x_hbm, g_hbm, gs_hbm, wq_hbm, wk_hbm, wv_hbm, wo_hbm, gain_hbm,
    x_first, grad_x,
    wbuf, theirs_v, xg, y_v, gs_v, gain_v,
    q_v, k_v, v_v, slope_q, slope_k, gn_v, attn_s, back_v, normed_v, dq_v, inner_v,
    st_src, st_in, st_pref, st_rs, st_row, st_po, st_p, state_v, early_v,
    own_v, core_out, core_in, hop_out, hop_in,
    loc_sem, sent, arrived,
):
    ctx = lax.axis_index("ctx")
    x = lax.axis_index("tp")
    c = ctx % 2
    z = (ctx // 2) % RING
    y = ctx // (2 * RING)

    def at(yy, zz):
        return ((yy * RING + zz) * 2 + c, x)

    def across(dev):
        return (dev[0] + 1 - 2 * c, x)

    peer = across((ctx, x))
    xr, xl, xo = (x + 1) % 4, (x + 3) % 4, (x + 2) % 4
    right, left = (ctx, xr), (ctx, xl)

    def remote(src, dst, ss, rs, dev):
        return pltpu.make_async_remote_copy(
            src_ref=src, dst_ref=dst, send_sem=ss, recv_sem=rs, device_id=dev, device_id_type=MESH
        )

    def send(src, dst, ss, rs, dev):
        remote(src, dst, ss, rs, dev).start()

    def arrive(dst, rs):
        remote(dst, dst, sent.at[0], rs, peer).wait_recv()

    def left_here(src, ss):
        remote(src, src, ss, arrived.at[0], peer).wait_send()

    barrier = pltpu.get_barrier_semaphore()
    partners = [peer, right, left]
    partners += [at(y, (z + d) % RING) for d in range(1, RING)]
    partners += [at((y + d) % RING, z) for d in range(1, RING)]
    partners += [across(dev) for dev in partners[3:]]
    for dev in partners:
        pl.semaphore_signal(barrier, inc=1, device_id=dev, device_id_type=MESH)

    mine = pl.ds(pl.multiple_of(c * 256, 256), 256)
    theirs = pl.ds(pl.multiple_of(256 - c * 256, 256), 256)
    shards = {K: wk_hbm, V: wv_hbm, Q: wq_hbm, O: wo_hbm}
    local = {}

    def stay(name, src, dst):
        local[name] = pltpu.make_async_copy(src, dst, loc_sem.at[len(local)])
        local[name].start()

    for w in (K, V, Q, O):
        stay(w, shards[w].at[:, mine], wbuf.at[w, y, z, c])
    for w in (K, V):
        stay((w, "theirs"), shards[w].at[:, theirs], theirs_v.at[w])
    stay("x", x_hbm, xg.at[0, x, 0])
    stay("g", g_hbm, xg.at[1, x, 0])
    stay("gain", gain_hbm, gain_v)
    stay("y", y_hbm, y_v)
    stay("gs", gs_hbm, gs_v)


    lo, hi = pl.ds(0, 64), pl.ds(64, 64)

    def x_hop(a, i, src, owner, part, dev):
        send(src.at[part], xg.at[a, owner, 0, part], sent.at[S_X + a], arrived.at[R_X + 6 * a + i], dev)

    def x_share(a, src, owner):
        send(src, xg.at[a, owner, 1], sent.at[S_XC + a], arrived.at[R_XC + a], peer)

    def x_here(a, i, owner, part):
        arrive(xg.at[a, owner, 0, part], arrived.at[R_X + 6 * a + i])

    def gather_x(a, src):
        x_hop(a, 0, src, x, lo, right)
        x_hop(a, 1, src, x, hi, left)
        x_hop(a, 2, src, x, hi, right)
        x_hop(a, 3, src, x, lo, left)
        x_share(a, src, x)

    def forward_x(a):
        x_here(a, 0, xl, lo)
        x_hop(a, 4, xg.at[a, xl, 0], xl, lo, right)
        x_here(a, 1, xr, hi)
        x_hop(a, 5, xg.at[a, xr, 0], xr, hi, left)

    def share_x(a):
        x_here(a, 2, xl, hi)
        x_share(a, xg.at[a, xl, 0], xl)
        x_here(a, 3, xr, lo)
        x_share(a, xg.at[a, xr, 0], xr)

    def last_x(a):
        x_here(a, 4, xo, lo)
        x_here(a, 5, xo, hi)
        x_share(a, xg.at[a, xo, 0], xo)

    def all_x(a):
        arrive(xg.at[a, :, 1], arrived.at[R_XC + a])

    def x_sent(a):
        left_here(xg.at[a, pl.ds(0, 3), 0], sent.at[S_X + a])
        left_here(xg.at[a, :, 1], sent.at[S_XC + a])

    def along_y(w):
        return w in (V, O)

    def first(w, shift):
        return at((y + shift) % RING, z) if along_y(w) else at(y, (z + shift) % RING)

    def second(w, shift):
        return at(y, (z + shift) % RING) if along_y(w) else at((y + shift) % RING, z)

    def block(w, one, two):
        if along_y(w):
            return wbuf.at[w, (y + one) % RING, (z + two) % RING]
        return wbuf.at[w, (y + two) % RING, (z + one) % RING]

    def shard_ready(w):
        local[w].wait()
        arrive(wbuf.at[w, y, z, 1 - c], arrived.at[R_SWAP + w])

    def spread(w):
        local[w].wait()
        local[w, "theirs"].wait()
        ref = wbuf.at[w, y, z, c]
        for d in FAR_FIRST:
            send(ref, ref, sent.at[S_FIRST + w], arrived.at[R_FIRST + w], first(w, d))
            send(theirs_v.at[w], ref, sent.at[S_FIRST + w], arrived.at[R_FIRST + w], across(first(w, d)))
        swap(w, theirs_v.at[w])

    def spread_done(w):
        arrive(wbuf.at[w, y, z, 1 - c], arrived.at[R_SWAP + w])
        arrive(wbuf.at[w, 0, pl.ds(0, 7)], arrived.at[R_FIRST + w])

    def ring_first(w, step):
        if step == 0:
            shard_ready(w)
        for way, sign in enumerate((-1, 1)):
            ref = block(w, (sign * step) % RING, 0)
            sem = R_FIRST + 2 + 8 * (w - Q) + 4 * way + step
            if step > 0:
                arrive(ref.at[way] if step == 4 else ref, arrived.at[sem - 1])
            if step < 4:
                out = ref.at[way] if step == 3 else ref
                send(out, out, sent.at[S_FIRST + w], arrived.at[sem], first(w, -sign))

    def chunk(w, part, two):
        size = 8 // CHUNKS[w]
        part = pl.ds(size * part, size)
        if along_y(w):
            return wbuf.at[w, part, (z + two) % RING]
        return wbuf.at[w, (y + two) % RING, part]

    def ring_second(w, step, i):
        count = CHUNKS[w]
        for way, sign in enumerate((-1, 1)):
            ref = chunk(w, count - 1 - i if way else i, (sign * step) % RING)
            sem = R_SECOND[w] + way * 7 * count // 2 + count * step + i
            if step > 0 and not (step == 4 and i >= count // 2):
                arrive(ref, arrived.at[sem - count])
            if step < 3 or (step == 3 and i < count // 2):
                send(ref, ref, sent.at[S_SECOND + w], arrived.at[sem], second(w, -sign))

    def weight_sent(w):
        left_here(wbuf.at[w, 0, pl.ds(0, 7)], sent.at[S_FIRST + w])
        left_here(wbuf.at[w, pl.ds(0, 7)], sent.at[S_SECOND + w])

    def exchange(turn, stage, src, dst, dev):
        index = 3 * turn + stage
        for d in FAR_FIRST:
            send(src(d), dst.at[turn, d], sent.at[S_STATE + index], arrived.at[R_STATE + index], dev(d))

    def exchanged(turn, stage, dst):
        arrive(dst.at[turn, pl.ds(1, 7)], arrived.at[R_STATE + 3 * turn + stage])

    def state_out(turn, states):
        for h in range(2):
            st_src[turn, :, h] = states[h].astype(BF16).reshape(RING, 16, HEAD)
        exchange(turn, 0, lambda d: st_src.at[turn, (z + d) % RING], st_in, lambda d: at(y, (z + d) % RING))
        st_in[turn, 0] = st_src[turn, z]

    def state_rows(turn):
        exchanged(turn, 0, st_in)
        total = jnp.zeros((2, 16, HEAD), F32)
        parts = []
        for i in range(RING) if turn == 0 else range(RING - 1, -1, -1):
            parts.append((i, total))
            total = total + st_in[turn, (z + RING - i) % RING].astype(F32)
        st_rs[turn] = total.astype(BF16)
        exchange(turn, 1, lambda d: st_rs.at[turn], st_row, lambda d: at((y + d) % RING, z))
        for i, part in parts:
            st_pref[i] = part

    def state_back(turn):
        exchanged(turn, 1, st_row)
        total = jnp.zeros((2, 16, HEAD), F32)
        for d in range(1, RING):
            use = (y >= d) if turn == 0 else (y < d)
            total = total + jnp.where(use, st_row[turn, d].astype(F32), 0.0)
        for i in range(RING):
            st_po[turn, i] = (total + st_pref[i]).astype(BF16)
        exchange(turn, 2, lambda d: st_po.at[turn, (z + d) % RING], st_p, lambda d: at(y, (z + d) % RING))
        st_p[turn, 0] = st_po[turn, z]

    def state_done(turn):
        exchanged(turn, 2, st_p)
        for j in range(RING):
            part = st_p[turn, (z + RING - j) % RING]
            for h in range(2):
                state_v[turn, h, pl.ds(16 * j, 16)] = part[h]

    def state(turn, h):
        return state_v[turn, h]

    def state_sent(turn):
        for stage in range(3):
            left_here(st_p.at[turn, pl.ds(1, 7)], sent.at[S_STATE + 3 * turn + stage])

    targets = {1: xr, 2: xo, 3: xl, 0: x}

    def rows_of(w, target):
        return wbuf[w, pl.ds(target * 2, 2)].reshape(512, 256)

    def sum_cores(a, product):
        for d in (2, 1, 3, 0):
            piece = product(d)
            core_out[a, d] = piece[128:].astype(BF16)
            send(core_out.at[a, d], core_in.at[a, d], sent.at[S_CORE + a], arrived.at[R_CORE + 4 * a + d], peer)
            own_v[d] = piece[:128]

    def both(a, d):
        arrive(core_in.at[a, d], arrived.at[R_CORE + 4 * a + d])
        return own_v[d] + core_in[a, d].astype(F32)

    def hop(a, d, part, dev, i):
        send(hop_out.at[a, d, part], hop_in.at[a, d, part], sent.at[S_HOP + a], arrived.at[R_HOP + 6 * a + i], dev)

    def landed(a, d, part, i):
        arrive(hop_in.at[a, d, part], arrived.at[R_HOP + 6 * a + i])

    def sum_first(a):
        hop_out[a, 2] = both(a, 2).astype(BF16)
        hop(a, 2, lo, right, 0)
        hop(a, 2, hi, left, 1)
        block = both(a, 1)
        hop_out[a, 1, 64:] = block[64:].astype(BF16)
        hop(a, 1, hi, right, 2)
        own_v[1] = block
        block = both(a, 3)
        hop_out[a, 3, :64] = block[:64].astype(BF16)
        hop(a, 3, lo, left, 3)
        own_v[3] = block

    def sum_second(a):
        landed(a, 2, lo, 0)
        hop_out[a, 1, :64] = (own_v[1, :64] + hop_in[a, 2, :64].astype(F32)).astype(BF16)
        hop(a, 1, lo, right, 4)
        landed(a, 2, hi, 1)
        hop_out[a, 3, 64:] = (own_v[3, 64:] + hop_in[a, 2, 64:].astype(F32)).astype(BF16)
        hop(a, 3, hi, left, 5)

    def sum_last(a):
        total = both(a, 0)
        landed(a, 1, hi, 2)
        landed(a, 3, lo, 3)
        landed(a, 1, lo, 4)
        landed(a, 3, hi, 5)
        return total + hop_in[a, 1].astype(F32) + hop_in[a, 3].astype(F32)

    def sums_sent(a):
        left_here(core_out.at[a], sent.at[S_CORE + a])
        left_here(hop_out.at[a, pl.ds(1, 3)], sent.at[S_HOP + a])

    def project(a, w):
        total = None
        for i in range(4):
            part = dot_nn(xg[a, i].reshape(256, 512), wbuf[w, 2 * i : 2 * i + 2].reshape(512, 256))
            total = part if total is None else total + part
        return total

    def feature(pre):
        return jnp.where(pre > 0, pre + 1.0, jnp.exp(jnp.minimum(pre, 0.0)))

    head = [slice(0, HEAD), slice(HEAD, 2 * HEAD)]
    place = [(lax.broadcasted_iota(jnp.int32, (256, 256), i) + c * 128) % 256 for i in range(2)]
    causal = place[0] >= place[1]

    pl.semaphore_wait(barrier, len(partners))

    def swap(w, src):
        send(src, wbuf.at[w, y, z, c], sent.at[S_SWAP], arrived.at[R_SWAP + w], peer)

    spread(K)
    spread(V)
    swap(Q, wq_hbm.at[:, theirs])
    swap(O, wo_hbm.at[:, theirs])
    gather_x(0, x_hbm)
    gather_x(1, g_hbm)

    def serve(pair, step):
        for i in range(CHUNKS[pair[0]]):
            for w in pair:
                ring_second(w, step, i)

    def serve_first(step):
        for w in (Q, O):
            ring_first(w, step)

    spread_done(K)
    spread_done(V)
    serve((K, V), 0)
    serve_first(0)
    forward_x(0)
    serve((K, V), 1)
    serve_first(1)
    share_x(0)
    serve((K, V), 2)
    serve_first(2)
    last_x(0)
    serve((K, V), 3)
    serve_first(3)
    serve_first(4)
    serve((Q, O), 0)
    local["x"].wait()
    all_x(0)
    serve((K, V), 4)
    feat = feature(project(0, K))
    slope_k[...] = jnp.minimum(feat, 1.0)
    k_v[...] = feat.astype(BF16)
    v_v[...] = project(0, V).astype(BF16)
    state_out(0, [dot_tn(k_v[:, s], v_v[:, s]) for s in head])
    serve((Q, O), 1)
    forward_x(1)
    share_x(1)
    state_rows(0)
    serve((Q, O), 2)
    last_x(1)
    state_back(0)
    serve((Q, O), 3)
    local["g"].wait()
    local["gain"].wait()
    all_x(1)
    serve((Q, O), 4)
    feat = feature(project(0, Q))
    slope_q[...] = jnp.minimum(feat, 1.0)
    q_v[...] = feat.astype(BF16)
    gain = jnp.where(c == 0, gain_v[:, :256], gain_v[:, 256:])
    gn_v[...] = project(1, O) * gain
    for h, s in enumerate(head):
        scores = jnp.where(causal, dot_nt(q_v[:, s], k_v[:, s]), 0.0).astype(BF16)
        attn_s[h] = scores
        inner_v[:, s] = dot_nn(scores, v_v[:, s])

    state_done(0)
    backs = []
    for h, s in enumerate(head):
        attn = inner_v[:, s] + dot_nn(q_v[:, s], state(0, h))
        scale = lax.rsqrt(jnp.mean(attn * attn, axis=-1, keepdims=True) + EPS)
        unit = attn * scale
        scaled = gn_v[:, s]
        back = ((scaled - unit * jnp.mean(unit * scaled, axis=-1, keepdims=True)) * scale).astype(BF16)
        back_v[:, s] = back
        backs.append(dot_tn(q_v[:, s], back))
        normed_v[:, s] = (unit * gain[:, s]).astype(BF16)
    state_out(1, backs)
    normed = normed_v[...]
    sum_cores(0, lambda d: dot_nt(normed, rows_of(O, targets[d])))
    sum_first(0)
    state_rows(1)
    for h, s in enumerate(head):
        back = back_v[:, s]
        gs = jnp.where(causal, dot_nt(back, v_v[:, s]), 0.0).astype(BF16)
        gq = dot_nn(gs, k_v[:, s]) + dot_nt(back, state(0, h))
        dq_v[0, :, s] = (gq * slope_q[:, s]).astype(BF16)
        gn_v[:, s] = dot_tn(gs, q_v[:, s])
        inner_v[:, s] = dot_tn(attn_s[h], back)
    state_back(1)
    sum_second(0)
    for d in range(4):
        early_v[d] = dot_nt(dq_v[0], rows_of(Q, targets[d]))
    local["y"].wait()
    x_first[...] = (y_v[...].astype(F32) - sum_last(0)).astype(BF16)
    left_here(wbuf.at[0, 0, pl.ds(0, 4), 0], sent.at[S_SWAP])
    for w in (K, V, Q, O):
        weight_sent(w)
    x_sent(0)
    x_sent(1)
    state_sent(0)
    sums_sent(0)

    state_done(1)
    for h, s in enumerate(head):
        later = state(1, h)
        gk = gn_v[:, s] + dot_nt(v_v[:, s], later)
        dq_v[1, :, s] = (gk * slope_k[:, s]).astype(BF16)
        dq_v[2, :, s] = (inner_v[:, s] + dot_nn(k_v[:, s], later)).astype(BF16)
    sum_cores(
        1,
        lambda d: early_v[d]
        + dot_nt(dq_v[1], rows_of(K, targets[d]))
        + dot_nt(dq_v[2], rows_of(V, targets[d])),
    )
    sum_first(1)
    sum_second(1)
    local["gs"].wait()
    grad_x[...] = (gs_v[...].astype(F32) + sum_last(1)).astype(BF16)
    state_sent(1)
    sums_sent(1)


def per_device(
    y_first, x_second, grad_first, grad_second, w_query, w_key, w_value, w_out, norm_gain
):
    dma = pltpu.SemaphoreType.DMA
    vm = pltpu.VMEM
    scratch = [
        vm((4, 8, 8, 2, 16, 256), BF16),
        vm((2, 16, 256), BF16),
        vm((2, 4, 2, 128, 512), BF16),
        vm((128, 512), BF16),
        vm((128, 512), BF16),
        vm((1, 512), F32),
        vm((256, 256), BF16),
        vm((256, 256), BF16),
        vm((256, 256), BF16),
        vm((256, 256), F32),
        vm((256, 256), F32),
        vm((256, 256), F32),
        vm((2, 256, 256), BF16),
        vm((256, 256), BF16),
        vm((256, 256), BF16),
        vm((3, 256, 256), BF16),
        vm((256, 256), F32),
        vm((2, 8, 2, 16, 128), BF16),
        vm((2, 8, 2, 16, 128), BF16),
        vm((8, 2, 16, 128), F32),
        vm((2, 2, 16, 128), BF16),
        vm((2, 8, 2, 16, 128), BF16),
        vm((2, 8, 2, 16, 128), BF16),
        vm((2, 8, 2, 16, 128), BF16),
        vm((2, 2, 128, 128), BF16),
        vm((4, 256, 512), F32),
        vm((4, 128, 512), F32),
        vm((2, 4, 128, 512), BF16),
        vm((2, 4, 128, 512), BF16),
        vm((2, 4, 128, 512), BF16),
        vm((2, 4, 128, 512), BF16),
        dma((11,)),
        dma((SENT,)),
        dma((ARRIVED,)),
    ]
    out = jax.ShapeDtypeStruct((128, 512), BF16)
    anywhere = pl.BlockSpec(memory_space=pl.ANY)
    return pl.pallas_call(
        kernel,
        out_shape=(out, out),
        in_specs=[anywhere] * 9,
        out_specs=(pl.BlockSpec(memory_space=pltpu.VMEM),) * 2,
        scratch_shapes=scratch,
        compiler_params=pltpu.CompilerParams(
            collective_id=0, has_side_effects=True, vmem_limit_bytes=63_400_000
        ),
        cost_estimate=pl.CostEstimate(
            flops=4_000_000_000, bytes_accessed=10_000_000, transcendentals=200_000
        ),
    )(
        y_first, x_second, grad_first, grad_second,
        w_query, w_key, w_value, w_out.T, norm_gain.reshape(1, 512),
    )


def solution(mesh):
    in_specs = (P("ctx", "tp"),) * 7 + (P("tp", "ctx"), P("tp"))
    out_specs = (P("ctx", "tp"), P("ctx", "tp"))
    return jax.shard_map(
        per_device, mesh=mesh, in_specs=in_specs, out_specs=out_specs, check_vma=False
    )
```

```python
import jax
import jax.numpy as jnp
from jax import lax
from jax.experimental import pallas as pl
from jax.experimental.pallas import tpu as pltpu
from jax.sharding import PartitionSpec as P

MESH = pl.DeviceIdType.MESH
F32 = jnp.float32
BF16 = jnp.bfloat16
HEAD = 128
EPS = 1e-06
RING = 8
K, V, Q, O = 0, 1, 2, 3
FAR_FIRST = (4, 3, 5, 2, 6, 1, 7)

S_SWAP, S_FIRST, S_SECOND, S_X, S_XC, S_STATE, S_CORE, S_HOP = 0, 1, 5, 9, 11, 13, 19, 21
SENT = 23
CHUNKS = (4, 4, 2, 2)
R_SECOND = (22, 50, 78, 92)
R_SWAP, R_FIRST, R_X, R_XC, R_STATE, R_CORE, R_HOP = 0, 4, 106, 118, 120, 126, 134
ARRIVED = 146


def dot_nn(a, b):
    return jnp.dot(a, b, preferred_element_type=F32)


def dot_nt(a, b):
    return lax.dot_general(a, b, (((1,), (1,)), ((), ())), preferred_element_type=F32)


def dot_tn(a, b):
    return lax.dot_general(a, b, (((0,), (0,)), ((), ())), preferred_element_type=F32)


def kernel(
    y_hbm, x_hbm, g_hbm, gs_hbm, wq_hbm, wk_hbm, wv_hbm, wo_hbm, gain_hbm,
    results,
    wbuf, theirs_v, xg, y_v, gs_v, gain_v,
    q_v, k_v, v_v, slope_q, slope_k, gn_v, attn_s, back_v, normed_v, dq_v, inner_v,
    st_src, st_in, st_pref, st_rs, st_row, st_po, st_p, state_v, early_v,
    own_v, core_out, core_in, hop_out, hop_in,
    loc_sem, sent, arrived,
):
    ctx = lax.axis_index("ctx")
    x = lax.axis_index("tp")
    c = ctx % 2
    z = (ctx // 2) % RING
    y = ctx // (2 * RING)

    def at(yy, zz):
        return ((yy * RING + zz) * 2 + c, x)

    def across(dev):
        return (dev[0] + 1 - 2 * c, x)

    peer = across((ctx, x))
    xr, xl, xo = (x + 1) % 4, (x + 3) % 4, (x + 2) % 4
    right, left = (ctx, xr), (ctx, xl)

    def remote(src, dst, ss, rs, dev):
        return pltpu.make_async_remote_copy(
            src_ref=src, dst_ref=dst, send_sem=ss, recv_sem=rs, device_id=dev, device_id_type=MESH
        )

    def send(src, dst, ss, rs, dev):
        remote(src, dst, ss, rs, dev).start()

    def arrive(dst, rs):
        remote(dst, dst, sent.at[0], rs, peer).wait_recv()

    def left_here(src, ss):
        remote(src, src, ss, arrived.at[0], peer).wait_send()

    barrier = pltpu.get_barrier_semaphore()
    partners = [peer, right, left]
    partners += [at(y, (z + d) % RING) for d in range(1, RING)]
    partners += [at((y + d) % RING, z) for d in range(1, RING)]
    partners += [across(dev) for dev in partners[3:]]
    for dev in partners:
        pl.semaphore_signal(barrier, inc=1, device_id=dev, device_id_type=MESH)

    mine = pl.ds(pl.multiple_of(c * 256, 256), 256)
    theirs = pl.ds(pl.multiple_of(256 - c * 256, 256), 256)
    shards = {K: wk_hbm, V: wv_hbm, Q: wq_hbm, O: wo_hbm}
    local = {}

    def stay(name, src, dst):
        local[name] = pltpu.make_async_copy(src, dst, loc_sem.at[len(local)])
        local[name].start()

    for w in (K, V, Q, O):
        stay(w, shards[w].at[:, mine], wbuf.at[w, y, z, c])
    for w in (K, V):
        stay((w, "theirs"), shards[w].at[:, theirs], theirs_v.at[w])
    stay("x", x_hbm, xg.at[0, x, 0])
    stay("g", g_hbm, xg.at[1, x, 0])
    stay("gain", gain_hbm, gain_v)
    stay("y", y_hbm, y_v)
    stay("gs", gs_hbm, gs_v)


    lo, hi = pl.ds(0, 64), pl.ds(64, 64)

    def x_hop(a, i, src, owner, part, dev):
        send(src.at[part], xg.at[a, owner, 0, part], sent.at[S_X + a], arrived.at[R_X + 6 * a + i], dev)

    def x_share(a, src, owner):
        send(src, xg.at[a, owner, 1], sent.at[S_XC + a], arrived.at[R_XC + a], peer)

    def x_here(a, i, owner, part):
        arrive(xg.at[a, owner, 0, part], arrived.at[R_X + 6 * a + i])

    def gather_x(a, src):
        x_hop(a, 0, src, x, lo, right)
        x_hop(a, 1, src, x, hi, left)
        x_hop(a, 2, src, x, hi, right)
        x_hop(a, 3, src, x, lo, left)
        x_share(a, src, x)

    def forward_x(a):
        x_here(a, 0, xl, lo)
        x_hop(a, 4, xg.at[a, xl, 0], xl, lo, right)
        x_here(a, 1, xr, hi)
        x_hop(a, 5, xg.at[a, xr, 0], xr, hi, left)

    def share_x(a):
        x_here(a, 2, xl, hi)
        x_share(a, xg.at[a, xl, 0], xl)
        x_here(a, 3, xr, lo)
        x_share(a, xg.at[a, xr, 0], xr)

    def last_x(a):
        x_here(a, 4, xo, lo)
        x_here(a, 5, xo, hi)
        x_share(a, xg.at[a, xo, 0], xo)

    def all_x(a):
        arrive(xg.at[a, :, 1], arrived.at[R_XC + a])

    def x_sent(a):
        left_here(xg.at[a, pl.ds(0, 3), 0], sent.at[S_X + a])
        left_here(xg.at[a, :, 1], sent.at[S_XC + a])

    def along_y(w):
        return w in (V, O)

    def first(w, shift):
        return at((y + shift) % RING, z) if along_y(w) else at(y, (z + shift) % RING)

    def second(w, shift):
        return at(y, (z + shift) % RING) if along_y(w) else at((y + shift) % RING, z)

    def block(w, one, two):
        if along_y(w):
            return wbuf.at[w, (y + one) % RING, (z + two) % RING]
        return wbuf.at[w, (y + two) % RING, (z + one) % RING]

    def shard_ready(w):
        local[w].wait()
        arrive(wbuf.at[w, y, z, 1 - c], arrived.at[R_SWAP + w])

    def spread(w):
        local[w].wait()
        local[w, "theirs"].wait()
        ref = wbuf.at[w, y, z, c]
        for d in FAR_FIRST:
            send(ref, ref, sent.at[S_FIRST + w], arrived.at[R_FIRST + w], first(w, d))
            send(theirs_v.at[w], ref, sent.at[S_FIRST + w], arrived.at[R_FIRST + w], across(first(w, d)))
        swap(w, theirs_v.at[w])

    def spread_done(w):
        arrive(wbuf.at[w, y, z, 1 - c], arrived.at[R_SWAP + w])
        arrive(wbuf.at[w, 0, pl.ds(0, 7)], arrived.at[R_FIRST + w])

    def ring_first(w, step):
        if step == 0:
            shard_ready(w)
        for way, sign in enumerate((-1, 1)):
            ref = block(w, (sign * step) % RING, 0)
            sem = R_FIRST + 2 + 8 * (w - Q) + 4 * way + step
            if step > 0:
                arrive(ref.at[way] if step == 4 else ref, arrived.at[sem - 1])
            if step < 4:
                out = ref.at[way] if step == 3 else ref
                send(out, out, sent.at[S_FIRST + w], arrived.at[sem], first(w, -sign))

    def chunk(w, part, two):
        size = 8 // CHUNKS[w]
        part = pl.ds(size * part, size)
        if along_y(w):
            return wbuf.at[w, part, (z + two) % RING]
        return wbuf.at[w, (y + two) % RING, part]

    def ring_second(w, step, i):
        count = CHUNKS[w]
        for way, sign in enumerate((-1, 1)):
            ref = chunk(w, count - 1 - i if way else i, (sign * step) % RING)
            sem = R_SECOND[w] + way * 7 * count // 2 + count * step + i
            if step > 0 and not (step == 4 and i >= count // 2):
                arrive(ref, arrived.at[sem - count])
            if step < 3 or (step == 3 and i < count // 2):
                send(ref, ref, sent.at[S_SECOND + w], arrived.at[sem], second(w, -sign))

    def weight_sent(w):
        left_here(wbuf.at[w, 0, pl.ds(0, 7)], sent.at[S_FIRST + w])
        left_here(wbuf.at[w, pl.ds(0, 7)], sent.at[S_SECOND + w])

    def exchange(turn, stage, src, dst, dev):
        index = 3 * turn + stage
        for d in FAR_FIRST:
            send(src(d), dst.at[turn, d], sent.at[S_STATE + index], arrived.at[R_STATE + index], dev(d))

    def exchanged(turn, stage, dst):
        arrive(dst.at[turn, pl.ds(1, 7)], arrived.at[R_STATE + 3 * turn + stage])

    def state_out(turn, states):
        for h in range(2):
            st_src[turn, :, h] = states[h].astype(BF16).reshape(RING, 16, HEAD)
        exchange(turn, 0, lambda d: st_src.at[turn, (z + d) % RING], st_in, lambda d: at(y, (z + d) % RING))
        st_in[turn, 0] = st_src[turn, z]

    def state_rows(turn):
        exchanged(turn, 0, st_in)
        total = jnp.zeros((2, 16, HEAD), F32)
        parts = []
        for i in range(RING) if turn == 0 else range(RING - 1, -1, -1):
            parts.append((i, total))
            total = total + st_in[turn, (z + RING - i) % RING].astype(F32)
        st_rs[turn] = total.astype(BF16)
        exchange(turn, 1, lambda d: st_rs.at[turn], st_row, lambda d: at((y + d) % RING, z))
        for i, part in parts:
            st_pref[i] = part

    def state_back(turn):
        exchanged(turn, 1, st_row)
        total = jnp.zeros((2, 16, HEAD), F32)
        for d in range(1, RING):
            use = (y >= d) if turn == 0 else (y < d)
            total = total + jnp.where(use, st_row[turn, d].astype(F32), 0.0)
        for i in range(RING):
            st_po[turn, i] = (total + st_pref[i]).astype(BF16)
        exchange(turn, 2, lambda d: st_po.at[turn, (z + d) % RING], st_p, lambda d: at(y, (z + d) % RING))
        st_p[turn, 0] = st_po[turn, z]

    def state_done(turn):
        exchanged(turn, 2, st_p)
        for j in range(RING):
            part = st_p[turn, (z + RING - j) % RING]
            for h in range(2):
                state_v[turn, h, pl.ds(16 * j, 16)] = part[h]

    def state(turn, h):
        return state_v[turn, h]

    def state_sent(turn):
        for stage in range(3):
            left_here(st_p.at[turn, pl.ds(1, 7)], sent.at[S_STATE + 3 * turn + stage])

    targets = {1: xr, 2: xo, 3: xl, 0: x}

    def rows_of(w, target):
        return wbuf[w, pl.ds(target * 2, 2)].reshape(512, 256)

    def sum_cores(a, product):
        for d in (2, 1, 3, 0):
            piece = product(d)
            core_out[a, d] = piece[128:].astype(BF16)
            send(core_out.at[a, d], core_in.at[a, d], sent.at[S_CORE + a], arrived.at[R_CORE + 4 * a + d], peer)
            own_v[d] = piece[:128]

    def both(a, d):
        arrive(core_in.at[a, d], arrived.at[R_CORE + 4 * a + d])
        return own_v[d] + core_in[a, d].astype(F32)

    def hop(a, d, part, dev, i):
        send(hop_out.at[a, d, part], hop_in.at[a, d, part], sent.at[S_HOP + a], arrived.at[R_HOP + 6 * a + i], dev)

    def landed(a, d, part, i):
        arrive(hop_in.at[a, d, part], arrived.at[R_HOP + 6 * a + i])

    def sum_first(a):
        hop_out[a, 2] = both(a, 2).astype(BF16)
        hop(a, 2, lo, right, 0)
        hop(a, 2, hi, left, 1)
        block = both(a, 1)
        hop_out[a, 1, 64:] = block[64:].astype(BF16)
        hop(a, 1, hi, right, 2)
        own_v[1] = block
        block = both(a, 3)
        hop_out[a, 3, :64] = block[:64].astype(BF16)
        hop(a, 3, lo, left, 3)
        own_v[3] = block

    def sum_second(a):
        landed(a, 2, lo, 0)
        hop_out[a, 1, :64] = (own_v[1, :64] + hop_in[a, 2, :64].astype(F32)).astype(BF16)
        hop(a, 1, lo, right, 4)
        landed(a, 2, hi, 1)
        hop_out[a, 3, 64:] = (own_v[3, 64:] + hop_in[a, 2, 64:].astype(F32)).astype(BF16)
        hop(a, 3, hi, left, 5)

    def sum_last(a):
        total = both(a, 0)
        landed(a, 1, hi, 2)
        landed(a, 3, lo, 3)
        landed(a, 1, lo, 4)
        landed(a, 3, hi, 5)
        return total + hop_in[a, 1].astype(F32) + hop_in[a, 3].astype(F32)

    def sums_sent(a):
        left_here(core_out.at[a], sent.at[S_CORE + a])
        left_here(hop_out.at[a, pl.ds(1, 3)], sent.at[S_HOP + a])

    def project(a, w):
        total = None
        for i in range(4):
            part = dot_nn(xg[a, i].reshape(256, 512), wbuf[w, 2 * i : 2 * i + 2].reshape(512, 256))
            total = part if total is None else total + part
        return total

    def feature(pre):
        return jnp.where(pre > 0, pre + 1.0, jnp.exp(jnp.minimum(pre, 0.0)))

    head = [slice(0, HEAD), slice(HEAD, 2 * HEAD)]
    place = [(lax.broadcasted_iota(jnp.int32, (256, 256), i) + c * 128) % 256 for i in range(2)]
    causal = place[0] >= place[1]

    pl.semaphore_wait(barrier, len(partners))

    def swap(w, src):
        send(src, wbuf.at[w, y, z, c], sent.at[S_SWAP], arrived.at[R_SWAP + w], peer)

    spread(K)
    spread(V)
    swap(Q, wq_hbm.at[:, theirs])
    swap(O, wo_hbm.at[:, theirs])
    gather_x(0, x_hbm)
    gather_x(1, g_hbm)

    def serve(pair, step):
        for i in range(CHUNKS[pair[0]]):
            for w in pair:
                ring_second(w, step, i)

    def serve_first(step):
        for w in (Q, O):
            ring_first(w, step)

    spread_done(K)
    spread_done(V)
    serve((K, V), 0)
    serve_first(0)
    forward_x(0)
    serve((K, V), 1)
    serve_first(1)
    share_x(0)
    serve((K, V), 2)
    serve_first(2)
    last_x(0)
    serve((K, V), 3)
    serve_first(3)
    serve_first(4)
    serve((Q, O), 0)
    local["x"].wait()
    all_x(0)
    serve((K, V), 4)
    feat = feature(project(0, K))
    slope_k[...] = jnp.minimum(feat, 1.0)
    k_v[...] = feat.astype(BF16)
    v_v[...] = project(0, V).astype(BF16)
    state_out(0, [dot_tn(k_v[:, s], v_v[:, s]) for s in head])
    serve((Q, O), 1)
    forward_x(1)
    share_x(1)
    state_rows(0)
    serve((Q, O), 2)
    last_x(1)
    state_back(0)
    serve((Q, O), 3)
    local["g"].wait()
    local["gain"].wait()
    all_x(1)
    serve((Q, O), 4)
    feat = feature(project(0, Q))
    slope_q[...] = jnp.minimum(feat, 1.0)
    q_v[...] = feat.astype(BF16)
    gain = jnp.where(c == 0, gain_v[:, :256], gain_v[:, 256:])
    gn_v[...] = project(1, O) * gain
    for h, s in enumerate(head):
        scores = jnp.where(causal, dot_nt(q_v[:, s], k_v[:, s]), 0.0).astype(BF16)
        attn_s[h] = scores
        inner_v[:, s] = dot_nn(scores, v_v[:, s])

    state_done(0)
    backs = []
    for h, s in enumerate(head):
        attn = inner_v[:, s] + dot_nn(q_v[:, s], state(0, h))
        scale = lax.rsqrt(jnp.mean(attn * attn, axis=-1, keepdims=True) + EPS)
        unit = attn * scale
        scaled = gn_v[:, s]
        back = ((scaled - unit * jnp.mean(unit * scaled, axis=-1, keepdims=True)) * scale).astype(BF16)
        back_v[:, s] = back
        backs.append(dot_tn(q_v[:, s], back))
        normed_v[:, s] = (unit * gain[:, s]).astype(BF16)
    state_out(1, backs)
    normed = normed_v[...]
    sum_cores(0, lambda d: dot_nt(normed, rows_of(O, targets[d])))
    sum_first(0)
    state_rows(1)
    for h, s in enumerate(head):
        back = back_v[:, s]
        gs = jnp.where(causal, dot_nt(back, v_v[:, s]), 0.0).astype(BF16)
        gq = dot_nn(gs, k_v[:, s]) + dot_nt(back, state(0, h))
        dq_v[0, :, s] = (gq * slope_q[:, s]).astype(BF16)
        gn_v[:, s] = dot_tn(gs, q_v[:, s])
        inner_v[:, s] = dot_tn(attn_s[h], back)
    state_back(1)
    sum_second(0)
    for d in range(4):
        early_v[d] = dot_nt(dq_v[0], rows_of(Q, targets[d]))
    local["y"].wait()
    y_v[...] = (y_v[...].astype(F32) - sum_last(0)).astype(BF16)
    stay("first", y_v, results.at[0])
    left_here(wbuf.at[0, 0, pl.ds(0, 4), 0], sent.at[S_SWAP])
    for w in (K, V, Q, O):
        weight_sent(w)
    x_sent(0)
    x_sent(1)
    state_sent(0)
    sums_sent(0)

    state_done(1)
    for h, s in enumerate(head):
        later = state(1, h)
        gk = gn_v[:, s] + dot_nt(v_v[:, s], later)
        dq_v[1, :, s] = (gk * slope_k[:, s]).astype(BF16)
        dq_v[2, :, s] = (inner_v[:, s] + dot_nn(k_v[:, s], later)).astype(BF16)
    sum_cores(
        1,
        lambda d: early_v[d]
        + dot_nt(dq_v[1], rows_of(K, targets[d]))
        + dot_nt(dq_v[2], rows_of(V, targets[d])),
    )
    sum_first(1)
    sum_second(1)
    local["gs"].wait()
    gs_v[...] = (gs_v[...].astype(F32) + sum_last(1)).astype(BF16)
    stay("second", gs_v, results.at[1])
    state_sent(1)
    sums_sent(1)
    local["first"].wait()
    local["second"].wait()


def per_device(
    y_first, x_second, grad_first, grad_second, w_query, w_key, w_value, w_out, norm_gain
):
    dma = pltpu.SemaphoreType.DMA
    vm = pltpu.VMEM
    scratch = [
        vm((4, 8, 8, 2, 16, 256), BF16),
        vm((2, 16, 256), BF16),
        vm((2, 4, 2, 128, 512), BF16),
        vm((128, 512), BF16),
        vm((128, 512), BF16),
        vm((1, 512), F32),
        vm((256, 256), BF16),
        vm((256, 256), BF16),
        vm((256, 256), BF16),
        vm((256, 256), F32),
        vm((256, 256), F32),
        vm((256, 256), F32),
        vm((2, 256, 256), BF16),
        vm((256, 256), BF16),
        vm((256, 256), BF16),
        vm((3, 256, 256), BF16),
        vm((256, 256), F32),
        vm((2, 8, 2, 16, 128), BF16),
        vm((2, 8, 2, 16, 128), BF16),
        vm((8, 2, 16, 128), F32),
        vm((2, 2, 16, 128), BF16),
        vm((2, 8, 2, 16, 128), BF16),
        vm((2, 8, 2, 16, 128), BF16),
        vm((2, 8, 2, 16, 128), BF16),
        vm((2, 2, 128, 128), BF16),
        vm((4, 256, 512), F32),
        vm((4, 128, 512), F32),
        vm((2, 4, 128, 512), BF16),
        vm((2, 4, 128, 512), BF16),
        vm((2, 4, 128, 512), BF16),
        vm((2, 4, 128, 512), BF16),
        dma((13,)),
        dma((SENT,)),
        dma((ARRIVED,)),
    ]
    out = jax.ShapeDtypeStruct((128, 512), BF16)
    anywhere = pl.BlockSpec(memory_space=pl.ANY)
    results = pl.pallas_call(
        kernel,
        out_shape=jax.ShapeDtypeStruct((2, 128, 512), BF16),
        in_specs=[anywhere] * 9,
        out_specs=anywhere,
        scratch_shapes=scratch,
        compiler_params=pltpu.CompilerParams(
            collective_id=0, has_side_effects=True, vmem_limit_bytes=63_400_000
        ),
        cost_estimate=pl.CostEstimate(
            flops=4_000_000_000, bytes_accessed=10_000_000, transcendentals=200_000
        ),
    )(
        y_first, x_second, grad_first, grad_second,
        w_query, w_key, w_value, w_out.T, norm_gain.reshape(1, 512),
    )
    return results[0], results[1]


def solution(mesh):
    in_specs = (P("ctx", "tp"),) * 7 + (P("tp", "ctx"), P("tp"))
    out_specs = (P("ctx", "tp"), P("ctx", "tp"))
    return jax.shard_map(
        per_device, mesh=mesh, in_specs=in_specs, out_specs=out_specs, check_vma=False
    )
```

```python
import jax
import jax.numpy as jnp
from jax import lax
from jax.experimental import pallas as pl
from jax.experimental.pallas import tpu as pltpu
from jax.sharding import PartitionSpec as P

MESH = pl.DeviceIdType.MESH
F32 = jnp.float32
BF16 = jnp.bfloat16
HEAD = 128
EPS = 1e-06
RING = 8
K, V, Q, O = 0, 1, 2, 3
FAR_FIRST = (4, 3, 5, 2, 6, 1, 7)

S_SWAP, S_FIRST, S_SECOND, S_X, S_XC, S_STATE, S_CORE, S_HOP = 0, 1, 5, 9, 11, 13, 19, 21
SENT = 23
CHUNKS = (4, 4, 2, 2)
R_SECOND = (22, 50, 78, 92)
R_SWAP, R_FIRST, R_X, R_XC, R_STATE, R_CORE, R_HOP = 0, 4, 106, 118, 120, 126, 134
ARRIVED = 146


def dot_nn(a, b):
    return jnp.dot(a, b, preferred_element_type=F32)


def dot_nt(a, b):
    return lax.dot_general(a, b, (((1,), (1,)), ((), ())), preferred_element_type=F32)


def dot_tn(a, b):
    return lax.dot_general(a, b, (((0,), (0,)), ((), ())), preferred_element_type=F32)


def kernel(
    y_hbm, x_hbm, g_hbm, gs_hbm, wq_hbm, wk_hbm, wv_hbm, wo_hbm, gain_hbm,
    results,
    wbuf, theirs_v, xg, y_v, gs_v, gain_v,
    q_v, k_v, v_v, slope_q, slope_k, gn_v, attn_s, back_v, normed_v, dq_v, inner_v,
    st_src, st_in, st_pref, st_rs, st_row, st_po, st_p, state_v, early_v,
    own_v, core_out, core_in, hop_out, hop_in,
    loc_sem, sent, arrived,
):
    ctx = lax.axis_index("ctx")
    x = lax.axis_index("tp")
    c = ctx % 2
    z = (ctx // 2) % RING
    y = ctx // (2 * RING)

    def at(yy, zz):
        return ((yy * RING + zz) * 2 + c, x)

    def across(dev):
        return (dev[0] + 1 - 2 * c, x)

    peer = across((ctx, x))
    xr, xl, xo = (x + 1) % 4, (x + 3) % 4, (x + 2) % 4
    right, left = (ctx, xr), (ctx, xl)

    def remote(src, dst, ss, rs, dev):
        return pltpu.make_async_remote_copy(
            src_ref=src, dst_ref=dst, send_sem=ss, recv_sem=rs, device_id=dev, device_id_type=MESH
        )

    def send(src, dst, ss, rs, dev):
        remote(src, dst, ss, rs, dev).start()

    def arrive(dst, rs):
        remote(dst, dst, sent.at[0], rs, peer).wait_recv()

    def left_here(src, ss):
        remote(src, src, ss, arrived.at[0], peer).wait_send()

    barrier = pltpu.get_barrier_semaphore()
    partners = []
    for d in FAR_FIRST:
        for dev in (at(y, (z + d) % RING), at((y + d) % RING, z)):
            partners += [dev, across(dev)]
    partners += [right, left, peer]
    for dev in partners:
        pl.semaphore_signal(barrier, inc=1, device_id=dev, device_id_type=MESH)

    mine = pl.ds(pl.multiple_of(c * 256, 256), 256)
    theirs = pl.ds(pl.multiple_of(256 - c * 256, 256), 256)
    shards = {K: wk_hbm, V: wv_hbm, Q: wq_hbm, O: wo_hbm}
    local = {}

    def stay(name, src, dst):
        local[name] = pltpu.make_async_copy(src, dst, loc_sem.at[len(local)])
        local[name].start()

    for w in (K, V, Q, O):
        stay(w, shards[w].at[:, mine], wbuf.at[w, y, z, c])
    for w in (K, V):
        stay((w, "theirs"), shards[w].at[:, theirs], theirs_v.at[w])
    stay("x", x_hbm, xg.at[0, x, 0])
    stay("g", g_hbm, xg.at[1, x, 0])
    stay("gain", gain_hbm, gain_v)
    stay("y", y_hbm, y_v)
    stay("gs", gs_hbm, gs_v)


    lo, hi = pl.ds(0, 64), pl.ds(64, 64)

    def x_hop(a, i, src, owner, part, dev):
        send(src.at[part], xg.at[a, owner, 0, part], sent.at[S_X + a], arrived.at[R_X + 6 * a + i], dev)

    def x_share(a, src, owner):
        send(src, xg.at[a, owner, 1], sent.at[S_XC + a], arrived.at[R_XC + a], peer)

    def x_here(a, i, owner, part):
        arrive(xg.at[a, owner, 0, part], arrived.at[R_X + 6 * a + i])

    def gather_x(a, src):
        x_hop(a, 0, src, x, lo, right)
        x_hop(a, 1, src, x, hi, left)
        x_hop(a, 2, src, x, hi, right)
        x_hop(a, 3, src, x, lo, left)
        x_share(a, src, x)

    def forward_x(a):
        x_here(a, 0, xl, lo)
        x_hop(a, 4, xg.at[a, xl, 0], xl, lo, right)
        x_here(a, 1, xr, hi)
        x_hop(a, 5, xg.at[a, xr, 0], xr, hi, left)

    def share_x(a):
        x_here(a, 2, xl, hi)
        x_share(a, xg.at[a, xl, 0], xl)
        x_here(a, 3, xr, lo)
        x_share(a, xg.at[a, xr, 0], xr)

    def last_x(a):
        x_here(a, 4, xo, lo)
        x_here(a, 5, xo, hi)
        x_share(a, xg.at[a, xo, 0], xo)

    def all_x(a):
        arrive(xg.at[a, :, 1], arrived.at[R_XC + a])

    def x_sent(a):
        left_here(xg.at[a, pl.ds(0, 3), 0], sent.at[S_X + a])
        left_here(xg.at[a, :, 1], sent.at[S_XC + a])

    def along_y(w):
        return w in (V, O)

    def first(w, shift):
        return at((y + shift) % RING, z) if along_y(w) else at(y, (z + shift) % RING)

    def second(w, shift):
        return at(y, (z + shift) % RING) if along_y(w) else at((y + shift) % RING, z)

    def block(w, one, two):
        if along_y(w):
            return wbuf.at[w, (y + one) % RING, (z + two) % RING]
        return wbuf.at[w, (y + two) % RING, (z + one) % RING]

    def shard_ready(w):
        local[w].wait()
        arrive(wbuf.at[w, y, z, 1 - c], arrived.at[R_SWAP + w])

    def spread(pair):
        for w in pair:
            local[w].wait()
            local[w, "theirs"].wait()
        for d in FAR_FIRST:
            for w in pair:
                ref = wbuf.at[w, y, z, c]
                sems = sent.at[S_FIRST + w], arrived.at[R_FIRST + w]
                send(ref, ref, *sems, first(w, d))
                send(theirs_v.at[w], ref, *sems, across(first(w, d)))
        for w in pair:
            swap(w, theirs_v.at[w])

    def spread_done(w):
        arrive(wbuf.at[w, y, z, 1 - c], arrived.at[R_SWAP + w])
        arrive(wbuf.at[w, 0, pl.ds(0, 7)], arrived.at[R_FIRST + w])

    def ring_first(w, step):
        if step == 0:
            shard_ready(w)
        for way, sign in enumerate((-1, 1)):
            ref = block(w, (sign * step) % RING, 0)
            sem = R_FIRST + 2 + 8 * (w - Q) + 4 * way + step
            if step > 0:
                arrive(ref.at[way] if step == 4 else ref, arrived.at[sem - 1])
            if step < 4:
                out = ref.at[way] if step == 3 else ref
                send(out, out, sent.at[S_FIRST + w], arrived.at[sem], first(w, -sign))

    def chunk(w, part, two):
        size = 8 // CHUNKS[w]
        part = pl.ds(size * part, size)
        if along_y(w):
            return wbuf.at[w, part, (z + two) % RING]
        return wbuf.at[w, (y + two) % RING, part]

    def ring_second(w, step, i):
        count = CHUNKS[w]
        for way, sign in enumerate((-1, 1)):
            ref = chunk(w, count - 1 - i if way else i, (sign * step) % RING)
            sem = R_SECOND[w] + way * 7 * count // 2 + count * step + i
            if step > 0 and not (step == 4 and i >= count // 2):
                arrive(ref, arrived.at[sem - count])
            if step < 3 or (step == 3 and i < count // 2):
                send(ref, ref, sent.at[S_SECOND + w], arrived.at[sem], second(w, -sign))

    def weight_sent(w):
        left_here(wbuf.at[w, 0, pl.ds(0, 7)], sent.at[S_FIRST + w])
        left_here(wbuf.at[w, pl.ds(0, 7)], sent.at[S_SECOND + w])

    def exchange(turn, stage, src, dst, dev):
        index = 3 * turn + stage
        for d in FAR_FIRST:
            send(src(d), dst.at[turn, d], sent.at[S_STATE + index], arrived.at[R_STATE + index], dev(d))

    def exchanged(turn, stage, dst):
        arrive(dst.at[turn, pl.ds(1, 7)], arrived.at[R_STATE + 3 * turn + stage])

    def state_out(turn, states):
        for h in range(2):
            st_src[turn, :, h] = states[h].astype(BF16).reshape(RING, 16, HEAD)
        exchange(turn, 0, lambda d: st_src.at[turn, (z + d) % RING], st_in, lambda d: at(y, (z + d) % RING))
        st_in[turn, 0] = st_src[turn, z]

    def state_rows(turn):
        exchanged(turn, 0, st_in)
        total = jnp.zeros((2, 16, HEAD), F32)
        parts = []
        for i in range(RING) if turn == 0 else range(RING - 1, -1, -1):
            parts.append((i, total))
            total = total + st_in[turn, (z + RING - i) % RING].astype(F32)
        st_rs[turn] = total.astype(BF16)
        exchange(turn, 1, lambda d: st_rs.at[turn], st_row, lambda d: at((y + d) % RING, z))
        for i, part in parts:
            st_pref[i] = part

    def state_back(turn):
        exchanged(turn, 1, st_row)
        total = jnp.zeros((2, 16, HEAD), F32)
        for d in range(1, RING):
            use = (y >= d) if turn == 0 else (y < d)
            total = total + jnp.where(use, st_row[turn, d].astype(F32), 0.0)
        for i in range(RING):
            st_po[turn, i] = (total + st_pref[i]).astype(BF16)
        exchange(turn, 2, lambda d: st_po.at[turn, (z + d) % RING], st_p, lambda d: at(y, (z + d) % RING))
        st_p[turn, 0] = st_po[turn, z]

    def state_done(turn):
        exchanged(turn, 2, st_p)
        for j in range(RING):
            part = st_p[turn, (z + RING - j) % RING]
            for h in range(2):
                state_v[turn, h, pl.ds(16 * j, 16)] = part[h]

    def state(turn, h):
        return state_v[turn, h]

    def state_sent(turn):
        for stage in range(3):
            left_here(st_p.at[turn, pl.ds(1, 7)], sent.at[S_STATE + 3 * turn + stage])

    targets = {1: xr, 2: xo, 3: xl, 0: x}

    def rows_of(w, target):
        return wbuf[w, pl.ds(target * 2, 2)].reshape(512, 256)

    def sum_cores(a, product):
        for d in (2, 1, 3, 0):
            piece = product(d)
            core_out[a, d] = piece[128:].astype(BF16)
            send(core_out.at[a, d], core_in.at[a, d], sent.at[S_CORE + a], arrived.at[R_CORE + 4 * a + d], peer)
            own_v[d] = piece[:128]

    def both(a, d):
        arrive(core_in.at[a, d], arrived.at[R_CORE + 4 * a + d])
        return own_v[d] + core_in[a, d].astype(F32)

    def hop(a, d, part, dev, i):
        send(hop_out.at[a, d, part], hop_in.at[a, d, part], sent.at[S_HOP + a], arrived.at[R_HOP + 6 * a + i], dev)

    def landed(a, d, part, i):
        arrive(hop_in.at[a, d, part], arrived.at[R_HOP + 6 * a + i])

    def sum_first(a):
        hop_out[a, 2] = both(a, 2).astype(BF16)
        hop(a, 2, lo, right, 0)
        hop(a, 2, hi, left, 1)
        block = both(a, 1)
        hop_out[a, 1, 64:] = block[64:].astype(BF16)
        hop(a, 1, hi, right, 2)
        own_v[1] = block
        block = both(a, 3)
        hop_out[a, 3, :64] = block[:64].astype(BF16)
        hop(a, 3, lo, left, 3)
        own_v[3] = block

    def sum_second(a):
        landed(a, 2, lo, 0)
        hop_out[a, 1, :64] = (own_v[1, :64] + hop_in[a, 2, :64].astype(F32)).astype(BF16)
        hop(a, 1, lo, right, 4)
        landed(a, 2, hi, 1)
        hop_out[a, 3, 64:] = (own_v[3, 64:] + hop_in[a, 2, 64:].astype(F32)).astype(BF16)
        hop(a, 3, hi, left, 5)

    def sum_last(a):
        total = both(a, 0)
        landed(a, 1, hi, 2)
        landed(a, 3, lo, 3)
        landed(a, 1, lo, 4)
        landed(a, 3, hi, 5)
        return total + hop_in[a, 1].astype(F32) + hop_in[a, 3].astype(F32)

    def sums_sent(a):
        left_here(core_out.at[a], sent.at[S_CORE + a])
        left_here(hop_out.at[a, pl.ds(1, 3)], sent.at[S_HOP + a])

    def project(a, w):
        total = None
        for i in range(4):
            part = dot_nn(xg[a, i].reshape(256, 512), wbuf[w, 2 * i : 2 * i + 2].reshape(512, 256))
            total = part if total is None else total + part
        return total

    def feature(pre):
        return jnp.where(pre > 0, pre + 1.0, jnp.exp(jnp.minimum(pre, 0.0)))

    head = [slice(0, HEAD), slice(HEAD, 2 * HEAD)]
    place = [(lax.broadcasted_iota(jnp.int32, (256, 256), i) + c * 128) % 256 for i in range(2)]
    causal = place[0] >= place[1]

    pl.semaphore_wait(barrier, len(partners))

    def swap(w, src):
        send(src, wbuf.at[w, y, z, c], sent.at[S_SWAP], arrived.at[R_SWAP + w], peer)

    spread((K, V))
    swap(Q, wq_hbm.at[:, theirs])
    swap(O, wo_hbm.at[:, theirs])
    gather_x(0, x_hbm)
    gather_x(1, g_hbm)

    def serve(pair, step):
        for i in range(CHUNKS[pair[0]]):
            for w in pair:
                ring_second(w, step, i)

    def serve_first(step):
        for w in (Q, O):
            ring_first(w, step)

    serve_first(0)
    spread_done(K)
    spread_done(V)
    serve((K, V), 0)
    serve_first(1)
    forward_x(0)
    serve((K, V), 1)
    serve_first(2)
    share_x(0)
    serve((K, V), 2)
    serve_first(3)
    last_x(0)
    serve((K, V), 3)
    serve_first(4)
    serve((Q, O), 0)
    local["x"].wait()
    all_x(0)
    serve((K, V), 4)
    feat = feature(project(0, K))
    slope_k[...] = jnp.minimum(feat, 1.0)
    k_v[...] = feat.astype(BF16)
    v_v[...] = project(0, V).astype(BF16)
    state_out(0, [dot_tn(k_v[:, s], v_v[:, s]) for s in head])
    serve((Q, O), 1)
    forward_x(1)
    share_x(1)
    state_rows(0)
    serve((Q, O), 2)
    last_x(1)
    state_back(0)
    serve((Q, O), 3)
    local["g"].wait()
    local["gain"].wait()
    all_x(1)
    serve((Q, O), 4)
    feat = feature(project(0, Q))
    slope_q[...] = jnp.minimum(feat, 1.0)
    q_v[...] = feat.astype(BF16)
    gain = jnp.where(c == 0, gain_v[:, :256], gain_v[:, 256:])
    gn_v[...] = project(1, O) * gain
    for h, s in enumerate(head):
        scores = jnp.where(causal, dot_nt(q_v[:, s], k_v[:, s]), 0.0).astype(BF16)
        attn_s[h] = scores
        inner_v[:, s] = dot_nn(scores, v_v[:, s])

    state_done(0)
    backs = []
    for h, s in enumerate(head):
        attn = inner_v[:, s] + dot_nn(q_v[:, s], state(0, h))
        scale = lax.rsqrt(jnp.mean(attn * attn, axis=-1, keepdims=True) + EPS)
        unit = attn * scale
        scaled = gn_v[:, s]
        back = ((scaled - unit * jnp.mean(unit * scaled, axis=-1, keepdims=True)) * scale).astype(BF16)
        back_v[:, s] = back
        backs.append(dot_tn(q_v[:, s], back))
        normed_v[:, s] = (unit * gain[:, s]).astype(BF16)
    state_out(1, backs)
    normed = normed_v[...]
    sum_cores(0, lambda d: dot_nt(normed, rows_of(O, targets[d])))
    sum_first(0)
    state_rows(1)
    for h, s in enumerate(head):
        back = back_v[:, s]
        gs = jnp.where(causal, dot_nt(back, v_v[:, s]), 0.0).astype(BF16)
        gq = dot_nn(gs, k_v[:, s]) + dot_nt(back, state(0, h))
        dq_v[0, :, s] = (gq * slope_q[:, s]).astype(BF16)
        gn_v[:, s] = dot_tn(gs, q_v[:, s])
        inner_v[:, s] = dot_tn(attn_s[h], back)
    state_back(1)
    sum_second(0)
    for d in range(4):
        early_v[d] = dot_nt(dq_v[0], rows_of(Q, targets[d]))
    local["y"].wait()
    y_v[...] = (y_v[...].astype(F32) - sum_last(0)).astype(BF16)
    stay("first", y_v, results.at[0])
    left_here(wbuf.at[0, 0, pl.ds(0, 4), 0], sent.at[S_SWAP])
    for w in (K, V, Q, O):
        weight_sent(w)
    x_sent(0)
    x_sent(1)
    state_sent(0)
    sums_sent(0)

    state_done(1)
    for h, s in enumerate(head):
        later = state(1, h)
        gk = gn_v[:, s] + dot_nt(v_v[:, s], later)
        dq_v[1, :, s] = (gk * slope_k[:, s]).astype(BF16)
        dq_v[2, :, s] = (inner_v[:, s] + dot_nn(k_v[:, s], later)).astype(BF16)
    sum_cores(
        1,
        lambda d: early_v[d]
        + dot_nt(dq_v[1], rows_of(K, targets[d]))
        + dot_nt(dq_v[2], rows_of(V, targets[d])),
    )
    sum_first(1)
    sum_second(1)
    local["gs"].wait()
    gs_v[...] = (gs_v[...].astype(F32) + sum_last(1)).astype(BF16)
    stay("second", gs_v, results.at[1])
    state_sent(1)
    sums_sent(1)
    local["first"].wait()
    local["second"].wait()


def per_device(
    y_first, x_second, grad_first, grad_second, w_query, w_key, w_value, w_out, norm_gain
):
    dma = pltpu.SemaphoreType.DMA
    vm = pltpu.VMEM
    scratch = [
        vm((4, 8, 8, 2, 16, 256), BF16),
        vm((2, 16, 256), BF16),
        vm((2, 4, 2, 128, 512), BF16),
        vm((128, 512), BF16),
        vm((128, 512), BF16),
        vm((1, 512), F32),
        vm((256, 256), BF16),
        vm((256, 256), BF16),
        vm((256, 256), BF16),
        vm((256, 256), F32),
        vm((256, 256), F32),
        vm((256, 256), F32),
        vm((2, 256, 256), BF16),
        vm((256, 256), BF16),
        vm((256, 256), BF16),
        vm((3, 256, 256), BF16),
        vm((256, 256), F32),
        vm((2, 8, 2, 16, 128), BF16),
        vm((2, 8, 2, 16, 128), BF16),
        vm((8, 2, 16, 128), F32),
        vm((2, 2, 16, 128), BF16),
        vm((2, 8, 2, 16, 128), BF16),
        vm((2, 8, 2, 16, 128), BF16),
        vm((2, 8, 2, 16, 128), BF16),
        vm((2, 2, 128, 128), BF16),
        vm((4, 256, 512), F32),
        vm((4, 128, 512), F32),
        vm((2, 4, 128, 512), BF16),
        vm((2, 4, 128, 512), BF16),
        vm((2, 4, 128, 512), BF16),
        vm((2, 4, 128, 512), BF16),
        dma((13,)),
        dma((SENT,)),
        dma((ARRIVED,)),
    ]
    out = jax.ShapeDtypeStruct((128, 512), BF16)
    anywhere = pl.BlockSpec(memory_space=pl.ANY)
    results = pl.pallas_call(
        kernel,
        out_shape=jax.ShapeDtypeStruct((2, 128, 512), BF16),
        in_specs=[anywhere] * 9,
        out_specs=anywhere,
        scratch_shapes=scratch,
        compiler_params=pltpu.CompilerParams(
            collective_id=0, has_side_effects=True, vmem_limit_bytes=63_400_000
        ),
        cost_estimate=pl.CostEstimate(
            flops=4_000_000_000, bytes_accessed=10_000_000, transcendentals=200_000
        ),
    )(
        y_first, x_second, grad_first, grad_second,
        w_query, w_key, w_value, w_out.T, norm_gain.reshape(1, 512),
    )
    return results[0], results[1]


def solution(mesh):
    in_specs = (P("ctx", "tp"),) * 7 + (P("tp", "ctx"), P("tp"))
    out_specs = (P("ctx", "tp"), P("ctx", "tp"))
    return jax.shard_map(
        per_device, mesh=mesh, in_specs=in_specs, out_specs=out_specs, check_vma=False
    )
```

```python
import jax
import jax.numpy as jnp
from jax import lax
from jax.experimental import pallas as pl
from jax.experimental.pallas import tpu as pltpu
from jax.sharding import PartitionSpec as P

MESH = pl.DeviceIdType.MESH
F32 = jnp.float32
BF16 = jnp.bfloat16
HEAD = 128
EPS = 1e-06
RING = 8
K, V, Q, O = 0, 1, 2, 3
FAR_FIRST = (4, 3, 5, 2, 6, 1, 7)

S_SWAP, S_FIRST, S_SECOND, S_X, S_XC, S_STATE, S_CORE, S_HOP = 0, 1, 5, 9, 11, 13, 19, 21
SENT = 23
CHUNKS = (4, 4, 2, 2)
R_SECOND = (22, 50, 78, 92)
R_SWAP, R_FIRST, R_X, R_XC, R_STATE, R_CORE, R_HOP = 0, 4, 106, 118, 120, 126, 134
ARRIVED = 146


def dot_nn(a, b):
    return jnp.dot(a, b, preferred_element_type=F32)


def dot_nt(a, b):
    return lax.dot_general(a, b, (((1,), (1,)), ((), ())), preferred_element_type=F32)


def dot_tn(a, b):
    return lax.dot_general(a, b, (((0,), (0,)), ((), ())), preferred_element_type=F32)


def kernel(
    y_hbm, x_hbm, g_hbm, gs_hbm, wq_hbm, wk_hbm, wv_hbm, wo_hbm, gain_hbm,
    results,
    wbuf, theirs_v, xg, y_v, gs_v, gain_v,
    q_v, k_v, v_v, slope_q, slope_k, gn_v, attn_s, back_v, normed_v, dq_v, inner_v,
    st_src, st_in, st_pref, st_rs, st_row, st_po, st_p, state_v, early_v,
    own_v, core_out, core_in, hop_out, hop_in,
    loc_sem, sent, arrived,
):
    ctx = lax.axis_index("ctx")
    x = lax.axis_index("tp")
    c = ctx % 2
    z = (ctx // 2) % RING
    y = ctx // (2 * RING)

    def at(yy, zz):
        return ((yy * RING + zz) * 2 + c, x)

    def across(dev):
        return (dev[0] + 1 - 2 * c, x)

    peer = across((ctx, x))
    xr, xl, xo = (x + 1) % 4, (x + 3) % 4, (x + 2) % 4
    right, left = (ctx, xr), (ctx, xl)

    def remote(src, dst, ss, rs, dev):
        return pltpu.make_async_remote_copy(
            src_ref=src, dst_ref=dst, send_sem=ss, recv_sem=rs, device_id=dev, device_id_type=MESH
        )

    def send(src, dst, ss, rs, dev):
        remote(src, dst, ss, rs, dev).start()

    def arrive(dst, rs):
        remote(dst, dst, sent.at[0], rs, peer).wait_recv()

    def left_here(src, ss):
        remote(src, src, ss, arrived.at[0], peer).wait_send()

    barrier = pltpu.get_barrier_semaphore()
    partners = []
    for d in FAR_FIRST:
        for dev in (at(y, (z + d) % RING), at((y + d) % RING, z)):
            partners += [dev, across(dev)]
    partners += [right, left, peer]
    for dev in partners:
        pl.semaphore_signal(barrier, inc=1, device_id=dev, device_id_type=MESH)

    mine = pl.ds(pl.multiple_of(c * 256, 256), 256)
    theirs = pl.ds(pl.multiple_of(256 - c * 256, 256), 256)
    shards = {K: wk_hbm, V: wv_hbm, Q: wq_hbm, O: wo_hbm}
    local = {}

    def stay(name, src, dst):
        local[name] = pltpu.make_async_copy(src, dst, loc_sem.at[len(local)])
        local[name].start()

    for w in (K, V, Q, O):
        stay(w, shards[w].at[:, mine], wbuf.at[w, y, z, c])
    for w in (K, V):
        stay((w, "theirs"), shards[w].at[:, theirs], theirs_v.at[w])
    stay("x", x_hbm, xg.at[0, x, 0])
    stay("g", g_hbm, xg.at[1, x, 0])
    stay("gain", gain_hbm, gain_v)
    stay("y", y_hbm, y_v)
    stay("gs", gs_hbm, gs_v)


    lo, hi = pl.ds(0, 64), pl.ds(64, 64)

    def x_hop(a, i, src, owner, part, dev):
        send(src.at[part], xg.at[a, owner, 0, part], sent.at[S_X + a], arrived.at[R_X + 6 * a + i], dev)

    def x_share(a, src, owner):
        send(src, xg.at[a, owner, 1], sent.at[S_XC + a], arrived.at[R_XC + a], peer)

    def x_here(a, i, owner, part):
        arrive(xg.at[a, owner, 0, part], arrived.at[R_X + 6 * a + i])

    def gather_x(a, src):
        x_hop(a, 0, src, x, lo, right)
        x_hop(a, 1, src, x, hi, left)
        x_hop(a, 2, src, x, hi, right)
        x_hop(a, 3, src, x, lo, left)
        x_share(a, src, x)

    def forward_x(a):
        x_here(a, 0, xl, lo)
        x_hop(a, 4, xg.at[a, xl, 0], xl, lo, right)
        x_here(a, 1, xr, hi)
        x_hop(a, 5, xg.at[a, xr, 0], xr, hi, left)

    def share_x(a):
        x_here(a, 2, xl, hi)
        x_share(a, xg.at[a, xl, 0], xl)
        x_here(a, 3, xr, lo)
        x_share(a, xg.at[a, xr, 0], xr)

    def last_x(a):
        x_here(a, 4, xo, lo)
        x_here(a, 5, xo, hi)
        x_share(a, xg.at[a, xo, 0], xo)

    def all_x(a):
        arrive(xg.at[a, :, 1], arrived.at[R_XC + a])

    def x_sent(a):
        left_here(xg.at[a, pl.ds(0, 3), 0], sent.at[S_X + a])
        left_here(xg.at[a, :, 1], sent.at[S_XC + a])

    def along_y(w):
        return w in (V, O)

    def first(w, shift):
        return at((y + shift) % RING, z) if along_y(w) else at(y, (z + shift) % RING)

    def second(w, shift):
        return at(y, (z + shift) % RING) if along_y(w) else at((y + shift) % RING, z)

    def block(w, one, two):
        if along_y(w):
            return wbuf.at[w, (y + one) % RING, (z + two) % RING]
        return wbuf.at[w, (y + two) % RING, (z + one) % RING]

    def shard_ready(w):
        local[w].wait()
        arrive(wbuf.at[w, y, z, 1 - c], arrived.at[R_SWAP + w])

    def spread(pair):
        for w in pair:
            local[w].wait()
            local[w, "theirs"].wait()
        for d in FAR_FIRST:
            for w in pair:
                ref = wbuf.at[w, y, z, c]
                sems = sent.at[S_FIRST + w], arrived.at[R_FIRST + w]
                send(ref, ref, *sems, first(w, d))
                send(theirs_v.at[w], ref, *sems, across(first(w, d)))
        for w in pair:
            swap(w, theirs_v.at[w])

    def spread_done(w):
        arrive(wbuf.at[w, y, z, 1 - c], arrived.at[R_SWAP + w])
        arrive(wbuf.at[w, 0, pl.ds(0, 7)], arrived.at[R_FIRST + w])

    def ring_first(w, step):
        if step == 0:
            shard_ready(w)
        for way, sign in enumerate((-1, 1)):
            ref = block(w, (sign * step) % RING, 0)
            sem = R_FIRST + 2 + 8 * (w - Q) + 4 * way + step
            if step > 0:
                arrive(ref.at[way] if step == 4 else ref, arrived.at[sem - 1])
            if step < 4:
                out = ref.at[way] if step == 3 else ref
                send(out, out, sent.at[S_FIRST + w], arrived.at[sem], first(w, -sign))

    def chunk(w, part, two):
        size = 8 // CHUNKS[w]
        part = pl.ds(size * part, size)
        if along_y(w):
            return wbuf.at[w, part, (z + two) % RING]
        return wbuf.at[w, (y + two) % RING, part]

    def ring_second(w, step, i):
        count = CHUNKS[w]
        for way, sign in enumerate((-1, 1)):
            ref = chunk(w, count - 1 - i if way else i, (sign * step) % RING)
            sem = R_SECOND[w] + way * 7 * count // 2 + count * step + i
            if step > 0 and not (step == 4 and i >= count // 2):
                arrive(ref, arrived.at[sem - count])
            if step < 3 or (step == 3 and i < count // 2):
                send(ref, ref, sent.at[S_SECOND + w], arrived.at[sem], second(w, -sign))

    def weight_sent(w):
        left_here(wbuf.at[w, 0, pl.ds(0, 7)], sent.at[S_FIRST + w])
        left_here(wbuf.at[w, pl.ds(0, 7)], sent.at[S_SECOND + w])

    def exchange(turn, stage, src, dst, dev):
        index = 3 * turn + stage
        for d in FAR_FIRST:
            send(src(d), dst.at[turn, d], sent.at[S_STATE + index], arrived.at[R_STATE + index], dev(d))

    def exchanged(turn, stage, dst):
        arrive(dst.at[turn, pl.ds(1, 7)], arrived.at[R_STATE + 3 * turn + stage])

    def state_out(turn, states):
        for h in range(2):
            st_src[turn, :, h] = states[h].astype(BF16).reshape(RING, 16, HEAD)
        exchange(turn, 0, lambda d: st_src.at[turn, (z + d) % RING], st_in, lambda d: at(y, (z + d) % RING))
        st_in[turn, 0] = st_src[turn, z]

    def state_rows(turn):
        exchanged(turn, 0, st_in)
        total = jnp.zeros((2, 16, HEAD), F32)
        parts = []
        for i in range(RING) if turn == 0 else range(RING - 1, -1, -1):
            parts.append((i, total))
            total = total + st_in[turn, (z + RING - i) % RING].astype(F32)
        st_rs[turn] = total.astype(BF16)
        exchange(turn, 1, lambda d: st_rs.at[turn], st_row, lambda d: at((y + d) % RING, z))
        for i, part in parts:
            st_pref[i] = part

    def state_back(turn):
        exchanged(turn, 1, st_row)
        total = jnp.zeros((2, 16, HEAD), F32)
        for d in range(1, RING):
            use = (y >= d) if turn == 0 else (y < d)
            total = total + jnp.where(use, st_row[turn, d].astype(F32), 0.0)
        for i in range(RING):
            st_po[turn, i] = (total + st_pref[i]).astype(BF16)
        exchange(turn, 2, lambda d: st_po.at[turn, (z + d) % RING], st_p, lambda d: at(y, (z + d) % RING))
        st_p[turn, 0] = st_po[turn, z]

    def state_done(turn):
        exchanged(turn, 2, st_p)
        for j in range(RING):
            part = st_p[turn, (z + RING - j) % RING]
            for h in range(2):
                state_v[turn, h, pl.ds(16 * j, 16)] = part[h]

    def state(turn, h):
        return state_v[turn, h]

    def state_sent(turn):
        for stage in range(3):
            left_here(st_p.at[turn, pl.ds(1, 7)], sent.at[S_STATE + 3 * turn + stage])

    targets = {1: xr, 2: xo, 3: xl, 0: x}

    def rows_of(w, target):
        return wbuf[w, pl.ds(target * 2, 2)].reshape(512, 256)

    def sum_cores(a, product):
        for d in (2, 1, 3, 0):
            piece = product(d)
            core_out[a, d] = piece[128:].astype(BF16)
            send(core_out.at[a, d], core_in.at[a, d], sent.at[S_CORE + a], arrived.at[R_CORE + 4 * a + d], peer)
            own_v[d] = piece[:128]

    def both(a, d):
        arrive(core_in.at[a, d], arrived.at[R_CORE + 4 * a + d])
        return own_v[d] + core_in[a, d].astype(F32)

    def hop(a, d, part, dev, i):
        send(hop_out.at[a, d, part], hop_in.at[a, d, part], sent.at[S_HOP + a], arrived.at[R_HOP + 6 * a + i], dev)

    def landed(a, d, part, i):
        arrive(hop_in.at[a, d, part], arrived.at[R_HOP + 6 * a + i])

    def sum_first(a):
        hop_out[a, 2] = both(a, 2).astype(BF16)
        hop(a, 2, lo, right, 0)
        hop(a, 2, hi, left, 1)
        block = both(a, 1)
        hop_out[a, 1, 64:] = block[64:].astype(BF16)
        hop(a, 1, hi, right, 2)
        own_v[1] = block
        block = both(a, 3)
        hop_out[a, 3, :64] = block[:64].astype(BF16)
        hop(a, 3, lo, left, 3)
        own_v[3] = block

    def sum_second(a):
        landed(a, 2, lo, 0)
        hop_out[a, 1, :64] = (own_v[1, :64] + hop_in[a, 2, :64].astype(F32)).astype(BF16)
        hop(a, 1, lo, right, 4)
        landed(a, 2, hi, 1)
        hop_out[a, 3, 64:] = (own_v[3, 64:] + hop_in[a, 2, 64:].astype(F32)).astype(BF16)
        hop(a, 3, hi, left, 5)

    def sum_last(a):
        total = both(a, 0)
        landed(a, 1, hi, 2)
        landed(a, 3, lo, 3)
        landed(a, 1, lo, 4)
        landed(a, 3, hi, 5)
        return total + hop_in[a, 1].astype(F32) + hop_in[a, 3].astype(F32)

    def sums_sent(a):
        left_here(core_out.at[a], sent.at[S_CORE + a])
        left_here(hop_out.at[a, pl.ds(1, 3)], sent.at[S_HOP + a])

    def project(a, w):
        total = None
        for i in range(4):
            part = dot_nn(xg[a, i].reshape(256, 512), wbuf[w, 2 * i : 2 * i + 2].reshape(512, 256))
            total = part if total is None else total + part
        return total

    def feature(pre):
        return jnp.where(pre > 0, pre + 1.0, jnp.exp(jnp.minimum(pre, 0.0)))

    head = [slice(0, HEAD), slice(HEAD, 2 * HEAD)]
    place = [(lax.broadcasted_iota(jnp.int32, (256, 256), i) + c * 128) % 256 for i in range(2)]
    causal = place[0] >= place[1]

    pl.semaphore_wait(barrier, len(partners))

    def swap(w, src):
        send(src, wbuf.at[w, y, z, c], sent.at[S_SWAP], arrived.at[R_SWAP + w], peer)

    spread((K, V))
    swap(Q, wq_hbm.at[:, theirs])
    swap(O, wo_hbm.at[:, theirs])
    gather_x(0, x_hbm)
    gather_x(1, g_hbm)

    def serve(pair, step):
        for i in range(CHUNKS[pair[0]]):
            for w in pair:
                ring_second(w, step, i)

    def serve_first(step):
        for w in (Q, O):
            ring_first(w, step)

    serve_first(0)
    spread_done(K)
    spread_done(V)
    serve((K, V), 0)
    serve_first(1)
    forward_x(0)
    serve((K, V), 1)
    serve_first(2)
    share_x(0)
    serve((K, V), 2)
    serve_first(3)
    last_x(0)
    serve((K, V), 3)
    serve_first(4)
    local["x"].wait()
    all_x(0)
    serve((K, V), 4)
    serve((Q, O), 0)
    feat = feature(project(0, K))
    slope_k[...] = jnp.minimum(feat, 1.0)
    k_v[...] = feat.astype(BF16)
    v_v[...] = project(0, V).astype(BF16)
    state_out(0, [dot_tn(k_v[:, s], v_v[:, s]) for s in head])
    serve((Q, O), 1)
    forward_x(1)
    share_x(1)
    state_rows(0)
    serve((Q, O), 2)
    last_x(1)
    state_back(0)
    serve((Q, O), 3)
    local["g"].wait()
    local["gain"].wait()
    all_x(1)
    serve((Q, O), 4)
    feat = feature(project(0, Q))
    slope_q[...] = jnp.minimum(feat, 1.0)
    q_v[...] = feat.astype(BF16)
    gain = jnp.where(c == 0, gain_v[:, :256], gain_v[:, 256:])
    gn_v[...] = project(1, O) * gain
    for h, s in enumerate(head):
        scores = jnp.where(causal, dot_nt(q_v[:, s], k_v[:, s]), 0.0).astype(BF16)
        attn_s[h] = scores
        inner_v[:, s] = dot_nn(scores, v_v[:, s])

    state_done(0)
    backs = []
    for h, s in enumerate(head):
        attn = inner_v[:, s] + dot_nn(q_v[:, s], state(0, h))
        scale = lax.rsqrt(jnp.mean(attn * attn, axis=-1, keepdims=True) + EPS)
        unit = attn * scale
        scaled = gn_v[:, s]
        back = ((scaled - unit * jnp.mean(unit * scaled, axis=-1, keepdims=True)) * scale).astype(BF16)
        back_v[:, s] = back
        backs.append(dot_tn(q_v[:, s], back))
        normed_v[:, s] = (unit * gain[:, s]).astype(BF16)
    state_out(1, backs)
    normed = normed_v[...]
    sum_cores(0, lambda d: dot_nt(normed, rows_of(O, targets[d])))
    sum_first(0)
    state_rows(1)
    for h, s in enumerate(head):
        back = back_v[:, s]
        gs = jnp.where(causal, dot_nt(back, v_v[:, s]), 0.0).astype(BF16)
        gq = dot_nn(gs, k_v[:, s]) + dot_nt(back, state(0, h))
        dq_v[0, :, s] = (gq * slope_q[:, s]).astype(BF16)
        gn_v[:, s] = dot_tn(gs, q_v[:, s])
        inner_v[:, s] = dot_tn(attn_s[h], back)
    state_back(1)
    sum_second(0)
    for d in range(4):
        early_v[d] = dot_nt(dq_v[0], rows_of(Q, targets[d]))
    local["y"].wait()
    y_v[...] = (y_v[...].astype(F32) - sum_last(0)).astype(BF16)
    stay("first", y_v, results.at[0])
    left_here(wbuf.at[0, 0, pl.ds(0, 4), 0], sent.at[S_SWAP])
    for w in (K, V, Q, O):
        weight_sent(w)
    x_sent(0)
    x_sent(1)
    state_sent(0)
    sums_sent(0)

    state_done(1)
    for h, s in enumerate(head):
        later = state(1, h)
        gk = gn_v[:, s] + dot_nt(v_v[:, s], later)
        dq_v[1, :, s] = (gk * slope_k[:, s]).astype(BF16)
        dq_v[2, :, s] = (inner_v[:, s] + dot_nn(k_v[:, s], later)).astype(BF16)
    sum_cores(
        1,
        lambda d: early_v[d]
        + dot_nt(dq_v[1], rows_of(K, targets[d]))
        + dot_nt(dq_v[2], rows_of(V, targets[d])),
    )
    sum_first(1)
    sum_second(1)
    local["gs"].wait()
    gs_v[...] = (gs_v[...].astype(F32) + sum_last(1)).astype(BF16)
    stay("second", gs_v, results.at[1])
    state_sent(1)
    sums_sent(1)
    local["first"].wait()
    local["second"].wait()


def per_device(
    y_first, x_second, grad_first, grad_second, w_query, w_key, w_value, w_out, norm_gain
):
    dma = pltpu.SemaphoreType.DMA
    vm = pltpu.VMEM
    scratch = [
        vm((4, 8, 8, 2, 16, 256), BF16),
        vm((2, 16, 256), BF16),
        vm((2, 4, 2, 128, 512), BF16),
        vm((128, 512), BF16),
        vm((128, 512), BF16),
        vm((1, 512), F32),
        vm((256, 256), BF16),
        vm((256, 256), BF16),
        vm((256, 256), BF16),
        vm((256, 256), F32),
        vm((256, 256), F32),
        vm((256, 256), F32),
        vm((2, 256, 256), BF16),
        vm((256, 256), BF16),
        vm((256, 256), BF16),
        vm((3, 256, 256), BF16),
        vm((256, 256), F32),
        vm((2, 8, 2, 16, 128), BF16),
        vm((2, 8, 2, 16, 128), BF16),
        vm((8, 2, 16, 128), F32),
        vm((2, 2, 16, 128), BF16),
        vm((2, 8, 2, 16, 128), BF16),
        vm((2, 8, 2, 16, 128), BF16),
        vm((2, 8, 2, 16, 128), BF16),
        vm((2, 2, 128, 128), BF16),
        vm((4, 256, 512), F32),
        vm((4, 128, 512), F32),
        vm((2, 4, 128, 512), BF16),
        vm((2, 4, 128, 512), BF16),
        vm((2, 4, 128, 512), BF16),
        vm((2, 4, 128, 512), BF16),
        dma((13,)),
        dma((SENT,)),
        dma((ARRIVED,)),
    ]
    out = jax.ShapeDtypeStruct((128, 512), BF16)
    anywhere = pl.BlockSpec(memory_space=pl.ANY)
    results = pl.pallas_call(
        kernel,
        out_shape=jax.ShapeDtypeStruct((2, 128, 512), BF16),
        in_specs=[anywhere] * 9,
        out_specs=anywhere,
        scratch_shapes=scratch,
        compiler_params=pltpu.CompilerParams(
            collective_id=0, has_side_effects=True, vmem_limit_bytes=63_400_000
        ),
        cost_estimate=pl.CostEstimate(
            flops=4_000_000_000, bytes_accessed=10_000_000, transcendentals=200_000
        ),
    )(
        y_first, x_second, grad_first, grad_second,
        w_query, w_key, w_value, w_out.T, norm_gain.reshape(1, 512),
    )
    return results[0], results[1]


def solution(mesh):
    in_specs = (P("ctx", "tp"),) * 7 + (P("tp", "ctx"), P("tp"))
    out_specs = (P("ctx", "tp"), P("ctx", "tp"))
    return jax.shard_map(
        per_device, mesh=mesh, in_specs=in_specs, out_specs=out_specs, check_vma=False
    )
```
